256 devices in a mesh: nodes: 16 (over z, core), feat: 16 (over y, x).
Axes of the slice: x: 4, y: 4, z: 8, core: 2. Of those that a mesh axis runs over, the one named last changes fastest.
Arguments:
- features: bfloat16 [262144, 1024], P('nodes', 'feat'), may hold values from -6 to 6
- tile_vals: bfloat16 [16, 16, 12, 128, 128], P('nodes'), may hold values from -0.375 to 0.375
- src_tile: int32 [16, 16, 12], P('nodes'), may hold values from 0 to 127
- dst_tile: int32 [16, 16, 12], P('nodes'), may hold values from 0 to 127
- counts: int32 [16, 16], P('nodes'), may hold values from 1 to 12, as said below
- weight: bfloat16 [2, 1024, 1024], replicated, may hold values from -0.125 to 0.125
Outputs:
- embedded: bfloat16 [262144, 1024], P('nodes', 'feat')
The draws below stay inside these ranges and needn't reach their ends.
Inputs may be any that keep to these rules, and one draw needn't show every extreme that they name: `counts`: in every draw one destination block receives 12 used slots from every source block.
All inputs are finite; a program needn't handle non-finite values.
Results may differ from the reference program's by a relative error of at most 0.0085.
Values may be sent and summed in bfloat16 or wider, within the bound.
A program may use at most 192 MiB of HBM per device.

```python
import jax
import jax.numpy as jnp
from jax import lax

D = 1024
TILE = 128
CAP = 12
NODE_DEV = 16384
NODES = 262144
N_NODES = 16


def draw_counts(key, part):
    key = jax.random.fold_in(key, 7)
    first, second = jax.random.split(key)
    base = jax.random.randint(first, (N_NODES, N_NODES), 1, CAP + 1)
    column = jax.random.randint(second, (), 0, N_NODES)
    full_column = jnp.arange(N_NODES)[None, :] == column
    return jnp.where(full_column, CAP, base).astype(jnp.int32)


def with_ends(values, key, smallest, largest):
    index_at = [jax.random.randint(jax.random.fold_in(key, axis), (), 0, length) for axis, length in enumerate(values.shape)]
    longest = values.shape.index(max(values.shape))
    beside = index_at[:longest] + [(index_at[longest] + 1) % values.shape[longest]] + index_at[longest + 1:]
    return values.at[tuple(index_at)].set(smallest).at[tuple(beside)].set(largest)


def levels(own_key, shape, cuts, low, largest):
    loudness = 1.0
    for dim, blocks in cuts:
        heights = jax.random.uniform(jax.random.fold_in(jax.random.fold_in(own_key, 6), dim), (blocks,), jnp.float32, low / len(cuts), largest / len(cuts))
        loudness = loudness * jnp.repeat(jnp.exp(heights), shape[dim] // blocks).reshape((-1,) + (1,) * (len(shape) - 1 - dim))
    return loudness


def noise(key, extent, width, bound, pieces=(), kind=jnp.bfloat16):
    entries = width * jax.random.normal(key, extent, jnp.float32)
    if pieces:
        entries = entries * levels(key, extent, pieces, -0.22, 0.18)
    return jnp.clip(entries, -bound, bound).astype(kind)


def setup_inputs(seed: int = 0) -> dict:
    arg_keys = jax.random.split(jax.random.key(seed), 7)
    features = noise(arg_keys[0], (NODES, D), 1.0, 6.0, ((0, 16), (1, 16)))
    tile_vals = noise(arg_keys[1], (N_NODES, N_NODES, CAP, TILE, TILE), (2 * TILE) ** -0.5, 0.375, ((0, 16),))
    src_tile = with_ends(jax.random.randint(arg_keys[2], (N_NODES, N_NODES, CAP), 0, NODE_DEV // TILE), jax.random.fold_in(arg_keys[2], 1), 0, (NODE_DEV // TILE) - 1).astype(jnp.int32)
    dst_tile = with_ends(jax.random.randint(arg_keys[3], (N_NODES, N_NODES, CAP), 0, NODE_DEV // TILE), jax.random.fold_in(arg_keys[3], 1), 0, (NODE_DEV // TILE) - 1).astype(jnp.int32)
    counts = draw_counts(jax.random.fold_in(arg_keys[6], 71), 0)
    weight = noise(arg_keys[5], (2, D, D), (2 * D) ** -0.5, 0.125)
    return {"features": features, "tile_vals": tile_vals, "src_tile": src_tile, "dst_tile": dst_tile, "counts": counts, "weight": weight}


def reference(features, tile_vals, src_tile, dst_tile, counts, weight):
    blocks = NODE_DEV // TILE
    panels = features.reshape(N_NODES, blocks, TILE, D)
    usable = jnp.arange(CAP, dtype=jnp.int32)[None, None, :] < counts[:, :, None]
    owner_index = jnp.broadcast_to(jnp.arange(N_NODES, dtype=jnp.int32)[:, None], (N_NODES, CAP))

    def one_source(aggregate, source):
        picked = panels[source][src_tile[source]]
        partial_value = jnp.einsum('dcij,dcjf->dcif', tile_vals[source].astype(jnp.float32), picked.astype(jnp.float32))
        partial_value = jnp.where(usable[source][:, :, None, None], partial_value, 0.0).astype(jnp.bfloat16)
        aggregate = aggregate.at[owner_index, dst_tile[source]].add(partial_value.astype(jnp.float32))
        return (aggregate, None)
    start_sum = jnp.zeros((N_NODES, blocks, TILE, D), jnp.float32)
    aggregate, unused = lax.scan(one_source, start_sum, jnp.arange(N_NODES, dtype=jnp.int32))
    aggregate = aggregate.reshape(N_NODES, NODE_DEV, D).astype(jnp.bfloat16)
    self_rows = features.reshape(N_NODES, NODE_DEV, D)

    def one_block(pair):
        hidden = jnp.dot(pair[0], weight[0], preferred_element_type=jnp.float32)
        hidden = hidden + jnp.dot(pair[1], weight[1], preferred_element_type=jnp.float32)
        active = jnp.maximum(hidden, 0.0)
        row_total = lax.optimization_barrier(jnp.sum(active * active, axis=1, keepdims=True))
        return (active * lax.rsqrt(row_total / D + 1e-06)).astype(jnp.bfloat16)
    embedded = lax.map(one_block, (aggregate, self_rows))
    return embedded.reshape(NODES, D)
```

```python
import jax
import jax.numpy as jnp
from jax import lax
from jax.experimental import pallas as pl
from jax.experimental.pallas import tpu as pltpu
from jax.sharding import PartitionSpec as P

MESH = pl.DeviceIdType.MESH
BF16, F32 = jnp.bfloat16, jnp.float32
N = 16
F = 16
CAP = 12
T = 128
TILES = 128
C = 64
D = 1024
K = 4
SHARE = 1024

NT = (((1,), (1,)), ((), ()))


def order(me, step):
    return lax.rem(me + step, 16)


def back_order(me, step):
    return lax.rem(me + 16 - step, 16)


def spread(into_chunks):
    a = lax.broadcasted_iota(jnp.int32, (512, 512), 0)
    b = lax.broadcasted_iota(jnp.int32, (512, 512), 1)
    nat, chunk = (a, b) if into_chunks else (b, a)
    tl, h, k, r = nat // 128, (nat // 64) % 2, (nat // 16) % 4, nat % 16
    return (chunk == k * 128 + h * 64 + tl * 16 + r).astype(F32).astype(BF16)


def kernel(
    src_ref,
    dmsg_ref,
    xt_ref,
    a_ref,
    w_ref,
    out_ref,
    xbuf,
    xtile,
    abuf,
    wbuf,
    wt0,
    wt1,
    zsend,
    zrecv,
    dtgt,
    r32,
    g32,
    asend,
    arecv,
    srecv,
    selfp,
    hs,
    lhs,
    act,
    bsend,
    brecv,
    perm,
    onehot,
    xsem,
    asem,
    wsem,
    own_sem,
    d_ss,
    d_rs,
    s_ss,
    s_rs,
    z_ss,
    z_rs,
    g_ss,
    g_rs,
    b_ss,
    b_rs,
):
    n, f = lax.axis_index("nodes"), lax.axis_index("feat")

    def node(i):
        return (i, f)

    def col(i):
        return (n, i)

    x_copy = pltpu.make_async_copy(xt_ref, xbuf, xsem)
    x_copy.start()

    def a_copy(step):
        d = order(n, step)
        return pltpu.make_async_copy(a_ref.at[d], abuf.at[d], asem.at[d])

    @pl.loop(0, 16)
    def _(step):
        a_copy(lax.rem(step + 1, 16)).start()

    w_copy = pltpu.make_async_copy(w_ref, wbuf, wsem)
    w_copy.start()

    barrier = pltpu.get_barrier_semaphore()

    @pl.loop(1, 16)
    def _(step):
        pl.semaphore_signal(barrier, inc=1, device_id=node(order(n, step)), device_id_type=MESH)
        pl.semaphore_signal(barrier, inc=1, device_id=col(order(f, step)), device_id_type=MESH)

    pl.semaphore_wait(barrier, 30)

    def d_send(to):
        return pltpu.make_async_remote_copy(
            dmsg_ref.at[to], dtgt.at[n], d_ss.at[to], d_rs.at[n], device_id=node(to), device_id_type=MESH
        )

    def d_recv(frm):
        return pltpu.make_async_remote_copy(
            dmsg_ref.at[frm], dtgt.at[frm], d_ss.at[frm], d_rs.at[frm], device_id=node(frm), device_id_type=MESH
        )

    def share(i):
        return pl.ds(pl.multiple_of(i * SHARE, SHARE), SHARE)

    def s_send(to):
        return pltpu.make_async_remote_copy(
            xt_ref.at[:, share(to)], srecv.at[f], s_ss.at[to], s_rs.at[f], device_id=col(to), device_id_type=MESH
        )

    def s_recv(frm):
        return pltpu.make_async_remote_copy(
            xt_ref.at[:, share(frm)], srecv.at[frm], s_ss.at[frm], s_rs.at[frm], device_id=col(frm), device_id_type=MESH
        )

    def z_send(k, to):
        return pltpu.make_async_remote_copy(
            zsend.at[k, to], zrecv.at[k, n], z_ss.at[k, to], z_rs.at[k, n], device_id=node(to), device_id_type=MESH
        )

    def z_recv(k, frm):
        return pltpu.make_async_remote_copy(
            zsend.at[k, frm], zrecv.at[k, frm], z_ss.at[k, frm], z_rs.at[k, frm], device_id=node(frm), device_id_type=MESH
        )

    def g_send(k, to):
        return pltpu.make_async_remote_copy(
            asend.at[k, to], arecv.at[k, f], g_ss.at[k, to], g_rs.at[k, f], device_id=col(to), device_id_type=MESH
        )

    def g_recv(k, frm):
        return pltpu.make_async_remote_copy(
            asend.at[k, frm], arecv.at[k, frm], g_ss.at[k, frm], g_rs.at[k, frm], device_id=col(frm), device_id_type=MESH
        )

    def rows(i):
        return pl.ds(pl.multiple_of(i * C, C), C)

    def b_send(k, to):
        return pltpu.make_async_remote_copy(
            bsend.at[k, rows(to)], brecv.at[k, rows(f)], b_ss.at[k, to], b_rs.at[k, f], device_id=col(to), device_id_type=MESH
        )

    def b_recv(k, frm):
        return pltpu.make_async_remote_copy(
            bsend.at[k, rows(frm)], brecv.at[k, rows(frm)], b_ss.at[k, frm], b_rs.at[k, frm], device_id=col(frm), device_id_type=MESH
        )

    @pl.loop(1, 16)
    def _(step):
        d_send(order(n, step)).start()
        s_send(order(f, step)).start()

    own_self = pltpu.make_async_copy(xt_ref.at[:, share(f)], srecv.at[f], own_sem)
    own_self.start()

    x_copy.wait()

    @pl.loop(0, TILES, unroll=8)
    def _(t):
        xtile[t] = xbuf[:, pl.ds(pl.multiple_of(t * T, T), T)]

    none = jnp.zeros((C, T), BF16)

    def products(d, put):
        for c in range(CAP):
            a = abuf[d, c]
            left = jnp.concatenate([a[: T // 2], a[T // 2 :]], axis=1)
            x = xtile[src_ref[c, d]]
            right = jnp.concatenate(
                [jnp.concatenate([x, none], axis=1), jnp.concatenate([none, x], axis=1)], axis=0
            )
            value = lax.dot_general(left, right, NT, preferred_element_type=F32).astype(BF16)
            for k in range(K):
                put(k, c, value[16 * k : 16 * k + 16])

    @pl.loop(1, 16)
    def _(step):
        d = order(n, step)
        a_copy(step).wait()

        def put(k, c, value):
            zsend[k, d, c] = value

        products(d, put)
        z_send(0, d).start()

    a_copy(0).wait()

    def put_own(k, c, value):
        zrecv[k, n, c] = value

    products(n, put_own)

    dtgt[n] = dmsg_ref[n]
    r32[...] = jnp.zeros_like(r32)
    perm[0] = spread(True)
    perm[1] = spread(False)
    w_copy.wait()

    for part, target in ((0, wt0), (1, wt1)):

        @pl.loop(0, 8)
        def _(i):
            at = pl.ds(pl.multiple_of(i * 128, 128), 128)
            for j in range(8):
                block = wbuf[part, at, 128 * j : 128 * j + 128]
                target[128 * j : 128 * j + 128, at] = block.T

    @pl.loop(1, 16)
    def _(step):
        d_recv(back_order(n, step)).wait_recv()

    low, high = dtgt[0], dtgt[8]
    for s in range(1, 8):
        low, high = low + dtgt[s], high + dtgt[8 + s]
    wanted = jnp.concatenate([low, high], axis=1)
    place = lax.broadcasted_iota(jnp.int32, (TILES, 256), 0) + 1
    onehot[...] = (place == wanted).astype(F32).astype(BF16)

    def self_part():
        own_self.wait()

        @pl.loop(1, 16)
        def _(step):
            s_recv(back_order(f, step)).wait_recv()

        @pl.loop(0, 4)
        def _(i):
            for tq in range(2):
                x = srecv[pl.ds(i * 4, 4), :, 512 * tq : 512 * tq + 512].reshape(256, 512)
                moved = jnp.dot(x, perm[0], preferred_element_type=F32).astype(BF16)
                for k in range(K):
                    selfp[k, pl.ds(pl.multiple_of(i * 256, 256), 256), 128 * tq : 128 * tq + 128] = moved[
                        :, 128 * k : 128 * k + 128
                    ]

        @pl.loop(0, K)
        def _(k):
            hs[k] = jnp.dot(wt1[...], selfp[k], preferred_element_type=F32)

    lane = lax.broadcasted_iota(jnp.int32, (T, 128), 1)

    def chunk(k, is_first, is_last):
        @pl.loop(0, 16)
        def _(step):
            s = back_order(n, step)

            @pl.when(step > 0)
            def _():
                z_recv(k, s).wait_recv()
                if not is_last:
                    z_send(k + 1, order(n, step)).start()

            for c in range(CAP):
                r32[pl.ds(s * 16 + c, 16, stride=256), :] = zrecv[k, s, c].astype(F32)

        @pl.loop(0, 16)
        def _(r):
            x = r32[pl.ds(pl.multiple_of(r * 256, 256), 256), :].astype(BF16)
            g32[pl.ds(r, TILES, stride=16), :] = jnp.dot(onehot[...], x, preferred_element_type=F32)

        @pl.loop(1, 16)
        def _(step):
            to = order(f, step)
            asend[k, to] = g32[pl.ds(pl.multiple_of(to * 128, 128), 128), :].astype(BF16)
            g_send(k, to).start()

        arecv[k, f] = g32[pl.ds(pl.multiple_of(f * 128, 128), 128), :].astype(BF16)

        if is_first:
            self_part()

        @pl.loop(1, 16)
        def _(step):
            g_recv(k, back_order(f, step)).wait_recv()

        for m in range(8):
            a, b = arecv[k, 2 * m].astype(F32), arecv[k, 2 * m + 1].astype(F32)
            first = jnp.where(lane < 64, a, pltpu.roll(b, 64, 1)).astype(BF16)
            second = jnp.where(lane < 64, pltpu.roll(a, 64, 1), b).astype(BF16)
            for tq in range(2):
                cols = slice(128 * m, 128 * m + 128)
                lhs[128 * tq : 128 * tq + 64, cols] = first[64 * tq : 64 * tq + 64]
                lhs[128 * tq + 64 : 128 * tq + 128, cols] = second[64 * tq : 64 * tq + 64]

        act[...] = jnp.maximum(hs[k] + lax.dot_general(wt0[...], lhs[...], NT, preferred_element_type=F32), 0.0)
        total = jnp.sum(act[...] * act[...], axis=0, keepdims=True)
        bsend[k] = (act[...] * lax.rsqrt(total / D + 1e-06)).astype(BF16)

        @pl.loop(1, 16)
        def _(step):
            b_send(k, order(f, step)).start()

        brecv[k, rows(f)] = bsend[k, rows(f)]

    chunk(0, True, False)

    @pl.loop(1, K - 1)
    def _(k):
        chunk(k, False, False)

    chunk(K - 1, False, True)

    @pl.loop(1, 16)
    def _(step):
        for k in range(K):
            b_recv(k, back_order(f, step)).wait_recv()

    @pl.loop(0, 4)
    def _(i):
        for tq in range(2):
            x = jnp.concatenate(
                [brecv[k, pl.ds(pl.multiple_of(i * 256, 256), 256), 128 * tq : 128 * tq + 128] for k in range(K)], axis=1
            )
            moved = jnp.dot(x, perm[1], preferred_element_type=F32).astype(BF16)
            for j in range(4):
                at = pl.multiple_of((i * 4 + j) * SHARE + 512 * tq, 512)
                out_ref[:, pl.ds(at, 512)] = moved[64 * j : 64 * j + 64]

    @pl.loop(1, 16)
    def _(step):
        d_send(order(n, step)).wait_send()
        s_send(order(f, step)).wait_send()
        for k in range(K):
            z_send(k, order(n, step)).wait_send()
            g_send(k, order(f, step)).wait_send()
            b_send(k, order(f, step)).wait_send()


def on_device(features, tile_vals, src_tile, dst_tile, counts, weight):
    n = lax.axis_index("nodes")
    xt = features.T
    src = src_tile.transpose(2, 0, 1).reshape(CAP, N)
    used = lax.broadcasted_iota(jnp.int32, (N, CAP), 1) < counts[0][:, None]
    target = jnp.pad(jnp.where(used, dst_tile[0] + 1, 0), ((0, 0), (0, 16 - CAP)))
    lanes = lax.broadcasted_iota(jnp.int32, (N, 128), 1)
    dmsg = jnp.where(lanes // 16 == n % 8, jnp.tile(target, (1, 8)), 0).reshape(N, 1, 128)

    hbm = pl.BlockSpec(memory_space=pl.ANY)
    vmem = pl.BlockSpec(memory_space=pltpu.VMEM)
    smem = pl.BlockSpec(memory_space=pltpu.SMEM)
    dma = pltpu.SemaphoreType.DMA
    out = pl.pallas_call(
        kernel,
        out_shape=jax.ShapeDtypeStruct((C, TILES * T), BF16),
        in_specs=[smem, vmem, hbm, hbm, hbm],
        out_specs=vmem,
        scratch_shapes=[
            pltpu.VMEM((C, TILES * T), BF16),
            pltpu.VMEM((TILES, C, T), BF16),
            pltpu.VMEM((N, CAP, T, T), BF16),
            pltpu.VMEM((2, D, D), BF16),
            pltpu.VMEM((D, D), BF16),
            pltpu.VMEM((D, D), BF16),
            pltpu.VMEM((K, N, CAP, 16, 128), BF16),
            pltpu.VMEM((K, N, CAP, 16, 128), BF16),
            pltpu.VMEM((N, 1, 128), jnp.int32),
            pltpu.VMEM((16 * 256, 128), F32),
            pltpu.VMEM((TILES * 16, 128), F32),
            pltpu.VMEM((K, F, 128, 128), BF16),
            pltpu.VMEM((K, F, 128, 128), BF16),
            pltpu.VMEM((F, C, SHARE), BF16),
            pltpu.VMEM((K, D, 256), BF16),
            pltpu.VMEM((K, D, 256), F32),
            pltpu.VMEM((256, D), BF16),
            pltpu.VMEM((D, 256), F32),
            pltpu.VMEM((K, D, 256), BF16),
            pltpu.VMEM((K, D, 256), BF16),
            pltpu.VMEM((2, 512, 512), BF16),
            pltpu.VMEM((TILES, 256), BF16),
            dma,
            dma((N,)),
            dma,
            dma,
            dma((N,)),
            dma((N,)),
            dma((F,)),
            dma((F,)),
            dma((K, N)),
            dma((K, N)),
            dma((K, F)),
            dma((K, F)),
            dma((K, F)),
            dma((K, F)),
        ],
        compiler_params=pltpu.CompilerParams(collective_id=1, has_side_effects=True, vmem_limit_bytes=60 * 2**20),
    )(src, dmsg, xt, tile_vals[0], weight)
    return out.T


def solution(mesh):
    return jax.shard_map(
        on_device,
        mesh=mesh,
        in_specs=(
            P("nodes", "feat"),
            P("nodes", None, None, None, None),
            P("nodes", None, None),
            P("nodes", None, None),
            P("nodes", None),
            P(),
        ),
        out_specs=P("nodes", "feat"),
        check_vma=False,
    )
```

```python
import jax
import jax.numpy as jnp
from jax import lax
from jax.experimental import pallas as pl
from jax.experimental.pallas import tpu as pltpu
from jax.sharding import PartitionSpec as P

MESH = pl.DeviceIdType.MESH
BF16, F32 = jnp.bfloat16, jnp.float32
N = 16
F = 16
CAP = 12
T = 128
TILES = 128
C = 64
D = 1024
SHARE = 1024
ROWS = (16, 16, 16, 8, 8)
A, B = 3, 2
LOOK = 2
LANES = 128 * (A + B)

NT = (((1,), (1,)), ((), ()))

FAR = sorted(
    [(dy, dx) for dy in range(4) for dx in range(4) if (dy, dx) != (0, 0)],
    key=lambda o: -(min(o[0], 4 - o[0]) + min(o[1], 4 - o[1])),
)


def node_partner(n, step, sign):
    j = lax.div(step, 2)
    dz = 4 + (2 * lax.rem(j, 2) - 1) * lax.div(j + 1, 2)
    return lax.rem(lax.div(n, 2) + 8 + sign * dz, 8) * 2 + lax.rem(n + step + 1, 2)


def feat_partner(f, offset):
    dy, dx = offset
    return lax.rem(lax.div(f, 4) + dy, 4) * 4 + lax.rem(lax.rem(f, 4) + dx, 4)


def placing(tq):
    lane = lax.broadcasted_iota(jnp.int32, (LANES, 512), 0)
    row = lax.broadcasted_iota(jnp.int32, (LANES, 512), 1)
    tl, h, i = row // 128, (row // 64) % 2, row % 64
    by16 = (i // 16) * 128 + h * 64 + tl * 16 + i % 16
    by8 = A * 128 + ((i - 16 * A) // 8) * 128 + tq * 64 + h * 32 + tl * 8 + i % 8
    return (lane == jnp.where(i < 16 * A, by16, by8)).astype(F32).astype(BF16)


def kernel(
    src_ref,
    dst_ref,
    counts_ref,
    xt_ref,
    a_ref,
    w_ref,
    out_a,
    out_b,
    out_perm,
    xbuf,
    xtile,
    abuf,
    wbuf,
    wt0,
    wt1,
    zsend_a,
    zsend_b,
    zrecv_a,
    zrecv_b,
    turn,
    dmsg,
    dtgt,
    r32,
    g32,
    asend_a,
    asend_b,
    arecv_a,
    arecv_b,
    srecv,
    selfp_a,
    selfp_b,
    hs_a,
    hs_b,
    lhs,
    act,
    bsend_a,
    bsend_b,
    perm,
    onehot,
    xsem,
    asem,
    wsem,
    own_sem,
    perm_sem,
    back_sem,
    d_ss,
    d_rs,
    s_ss,
    s_rs,
    z_ss,
    z_rs,
    g_ss,
    g_rs,
    b_ss,
    b_rs,
):
    n, f = lax.axis_index("nodes"), lax.axis_index("feat")
    across = [feat_partner(f, o) for o in FAR]

    def node(i):
        return (i, f)

    def col(i):
        return (n, i)

    def to_node(step):
        return node_partner(n, step, 1)

    def from_node(step):
        return node_partner(n, step, -1)

    def part(a, b, k):
        return a.at[k] if k < A else b.at[k - A]

    x_copy = pltpu.make_async_copy(xt_ref, xbuf, xsem)
    x_copy.start()

    def a_copy(d):
        return pltpu.make_async_copy(a_ref.at[d], abuf.at[d], asem.at[d])

    @pl.loop(0, 16)
    def _(step):
        a_copy(to_node(step)).start()

    w_copy = pltpu.make_async_copy(w_ref, wbuf, wsem)
    w_copy.start()

    barrier = pltpu.get_barrier_semaphore()

    @pl.loop(0, 15)
    def _(step):
        pl.semaphore_signal(barrier, inc=1, device_id=node(to_node(step)), device_id_type=MESH)

    for to in across:
        pl.semaphore_signal(barrier, inc=1, device_id=col(to), device_id_type=MESH)

    x_copy.wait()

    @pl.loop(0, TILES, unroll=8)
    def _(t):
        xtile[t] = xbuf[:, pl.ds(pl.multiple_of(t * T, T), T)]

    def remote(src, dst, ss, rs, device):
        return pltpu.make_async_remote_copy(src, dst, ss, rs, device_id=device, device_id_type=MESH)

    def all_of(ref, size=1):
        return ref.at[pl.ds(0, 15 * size)]

    def d_send(to):
        return remote(dmsg.at[to], dtgt.at[n], d_ss, d_rs, node(to))

    def d_all():
        return remote(all_of(dmsg), all_of(dtgt), d_ss, d_rs, node(n))

    def share(i):
        return pl.ds(pl.multiple_of(i * SHARE, SHARE), SHARE)

    def s_send(to):
        return remote(xt_ref.at[:, share(to)], srecv.at[f], s_ss, s_rs, col(to))

    def s_all():
        return remote(all_of(srecv), all_of(srecv), s_ss, s_rs, col(f))

    def z_send(k, to):
        src, dst = part(zsend_a, zsend_b, k), part(zrecv_a, zrecv_b, k)
        return remote(src.at[to], dst.at[n], z_ss.at[k], z_rs.at[k, n], node(to))

    def z_recv(k, frm):
        src, dst = part(zsend_a, zsend_b, k), part(zrecv_a, zrecv_b, k)
        return remote(src.at[frm], dst.at[frm], z_ss.at[k], z_rs.at[k, frm], node(frm))

    def z_all(k):
        src, dst = part(zsend_a, zsend_b, k), part(zrecv_a, zrecv_b, k)
        return remote(all_of(src), all_of(dst), z_ss.at[k], z_rs.at[k, n], node(n))

    def g_send(k, to):
        src, dst = part(asend_a, asend_b, k), part(arecv_a, arecv_b, k)
        return remote(src.at[to], dst.at[f], g_ss.at[k], g_rs.at[k], col(to))

    def g_all(k):
        src, dst = part(asend_a, asend_b, k), part(arecv_a, arecv_b, k)
        return remote(all_of(src), all_of(dst), g_ss.at[k], g_rs.at[k], col(f))

    def rows(i):
        return pl.ds(pl.multiple_of(i * C, C), C)

    def b_send(k, to):
        src, dst = part(bsend_a, bsend_b, k), part(out_a, out_b, k)
        return remote(src.at[rows(to)], dst.at[rows(f)], b_ss.at[k], b_rs.at[k], col(to))

    def b_all(k):
        src, dst = part(bsend_a, bsend_b, k), part(out_a, out_b, k)
        return remote(all_of(src, C), all_of(dst, C), b_ss.at[k], b_rs.at[k], col(f))

    def b_own(k):
        src, dst = part(bsend_a, bsend_b, k), part(out_a, out_b, k)
        return pltpu.make_async_copy(src.at[rows(f)], dst.at[rows(f)], back_sem.at[k])

    none = jnp.zeros((C, T), BF16)

    def products(d, to_a, to_b, at):
        kept = None
        for c in range(CAP):
            a = abuf[d, c]
            left = jnp.concatenate([a[: T // 2], a[T // 2 :]], axis=1)
            x = xtile[src_ref[c, 0, d]]
            right = jnp.concatenate(
                [jnp.concatenate([x, none], axis=1), jnp.concatenate([none, x], axis=1)], axis=0
            )
            value = lax.dot_general(left, right, NT, preferred_element_type=F32)
            for k in range(A):
                to_a[k, at, c] = value[16 * k : 16 * k + 16].astype(BF16)
            if c % 2 == 0:
                kept = value
                continue
            for k in range(B):
                rows8 = slice(16 * A + 8 * k, 16 * A + 8 * k + 8)
                to_b[k, at, c // 2] = jnp.concatenate([kept[rows8], value[rows8]], axis=0).astype(BF16)

    def stage_one(step):
        d = to_node(step)
        a_copy(d).wait()
        products(d, zsend_a, zsend_b, d)

    stage_one(0)
    stage_one(1)
    pl.semaphore_wait(barrier, 30)
    for step in range(2):
        z_send(0, to_node(step)).start()

    for to in across:
        s_send(to).start()

    own_self = pltpu.make_async_copy(xt_ref.at[:, share(f)], srecv.at[f], own_sem)
    own_self.start()

    @pl.loop(2, 15)
    def _(step):
        stage_one(step)
        z_send(0, to_node(step)).start()

    turn[...] = jnp.zeros_like(turn)
    for c in range(CAP):
        used = jnp.where(counts_ref[...] > c, dst_ref[c] + 1, 0)
        turn[pl.ds(16 * (n % 8) + c, 1), 0:N] = used.astype(F32)
    turned = turn[...].T
    for d in range(N):
        dmsg[d] = turned[d : d + 1].astype(jnp.int32)

    @pl.loop(0, 15)
    def _(step):
        d_send(to_node(step)).start()

    for k in range(1, LOOK):

        @pl.loop(0, 15)
        def _(step):
            z_send(k, to_node(step)).start()

    a_copy(n).wait()
    products(n, zrecv_a, zrecv_b, n)

    dtgt[n] = dmsg[n]
    r32[...] = jnp.zeros_like(r32)
    perm[0] = placing(0)
    perm[1] = placing(1)
    perm_copy = pltpu.make_async_copy(perm, out_perm, perm_sem)
    perm_copy.start()
    w_copy.wait()

    for which, target in ((0, wt0), (1, wt1)):

        @pl.loop(0, 8)
        def _(i):
            at = pl.ds(pl.multiple_of(i * 128, 128), 128)
            for j in range(8):
                block = wbuf[which, at, 128 * j : 128 * j + 128]
                target[128 * j : 128 * j + 128, at] = block.T

    d_all().wait_recv()
    low, high = dtgt[0], dtgt[8]
    for s in range(1, 8):
        low, high = low + dtgt[s], high + dtgt[8 + s]
    wanted = jnp.concatenate([low, high], axis=1)
    place = lax.broadcasted_iota(jnp.int32, (TILES, 256), 0) + 1
    onehot[...] = (place == wanted).astype(F32).astype(BF16)

    def aggregate(k):
        nr = ROWS[k]
        got = part(zrecv_a, zrecv_b, k)

        def unpack(s):
            if nr == 16:
                for c in range(CAP):
                    r32[pl.ds(s * 16 + c, 16, stride=256), :] = got[s, c].astype(F32)
            else:
                for c in range(0, CAP, 2):
                    both = got[s, c // 2].astype(F32)
                    r32[pl.ds(s * 16 + c, 8, stride=256), :] = both[:8]
                    r32[pl.ds(s * 16 + c + 1, 8, stride=256), :] = both[8:]

        unpack(n)

        @pl.loop(0, 15)
        def _(step):
            s = from_node(step)
            z_recv(k, s).wait_recv()
            if k + LOOK < len(ROWS):
                z_send(k + LOOK, to_node(step)).start()
            unpack(s)

        @pl.loop(0, nr)
        def _(r):
            x = r32[pl.ds(pl.multiple_of(r * 256, 256), 256), :].astype(BF16)
            g32[pl.ds(r, TILES, stride=nr), :] = jnp.dot(onehot[...], x, preferred_element_type=F32)

        def packed(i):
            return g32[pl.ds(pl.multiple_of(i * 8 * nr, 8 * nr), 8 * nr), :].astype(BF16)

        out, mine = part(asend_a, asend_b, k), part(arecv_a, arecv_b, k)
        for to in across:
            out[to] = packed(to)
            g_send(k, to).start()
        mine[f] = packed(f)

    def self_part():
        own_self.wait()
        s_all().wait_recv()

        @pl.loop(0, 4)
        def _(i):
            at = pl.ds(pl.multiple_of(i * 256, 256), 256)
            by8 = [0.0] * B
            for tq in range(2):
                x = srecv[pl.ds(i * 4, 4), :, 512 * tq : 512 * tq + 512].reshape(256, 512)
                moved = lax.dot_general(x, perm[tq], NT, preferred_element_type=F32)
                for k in range(A):
                    selfp_a[k, at, 128 * tq : 128 * tq + 128] = moved[:, 128 * k : 128 * k + 128].astype(BF16)
                for k in range(B):
                    by8[k] = by8[k] + moved[:, 128 * (A + k) : 128 * (A + k) + 128]
            for k in range(B):
                selfp_b[k, at, :] = by8[k].astype(BF16)

        for k in range(A):
            hs_a[k] = jnp.dot(wt1[...], selfp_a[k], preferred_element_type=F32)
        for k in range(B):
            hs_b[k] = jnp.dot(wt1[...], selfp_b[k], preferred_element_type=F32)

    def layer(k):
        nr = ROWS[k]
        wide = 16 * nr
        g_all(k).wait_recv()
        got = part(arecv_a, arecv_b, k)
        lane = lax.broadcasted_iota(jnp.int32, (8 * nr, 128), 1)
        for m in range(8):
            a, b = got[2 * m].astype(F32), got[2 * m + 1].astype(F32)
            first = jnp.where(lane < 64, a, pltpu.roll(b, 64, 1)).astype(BF16)
            second = jnp.where(lane < 64, pltpu.roll(a, 64, 1), b).astype(BF16)
            cols = slice(128 * m, 128 * m + 128)
            for tq in range(2):
                at, of = 8 * nr * tq, slice(4 * nr * tq, 4 * nr * tq + 4 * nr)
                lhs[at : at + 4 * nr, cols] = first[of]
                lhs[at + 4 * nr : at + 8 * nr, cols] = second[of]

        here, away = part(hs_a, hs_b, k), part(bsend_a, bsend_b, k)
        hidden = here[...] + lax.dot_general(wt0[...], lhs[0:wide], NT, preferred_element_type=F32)
        act[:, 0:wide] = jnp.maximum(hidden, 0.0)
        total = jnp.sum(act[:, 0:wide] * act[:, 0:wide], axis=0, keepdims=True)
        away[...] = (act[:, 0:wide] * lax.rsqrt(total / D + 1e-06)).astype(BF16)
        for to in across:
            b_send(k, to).start()
        b_own(k).start()

    for k in range(len(ROWS)):
        aggregate(k)
        if k == 0:
            self_part()
        layer(k)

    perm_copy.wait()
    d_all().wait_send()
    s_all().wait_send()
    for k in range(len(ROWS)):
        z_all(k).wait_send()
        g_all(k).wait_send()
        b_all(k).wait_send()
        b_own(k).wait()
        b_all(k).wait_recv()


def place_kernel(a_ref, b_ref, perm_ref, out_ref):
    for tq in range(2):
        x = [a_ref[k, :, 128 * tq : 128 * tq + 128] for k in range(A)] + [b_ref[k] for k in range(B)]
        moved = jnp.dot(jnp.concatenate(x, axis=1), perm_ref[tq], preferred_element_type=F32).astype(BF16)
        for j in range(4):
            out_ref[:, SHARE * j + 512 * tq : SHARE * j + 512 * tq + 512] = moved[C * j : C * j + C]


def on_device(features, tile_vals, src_tile, dst_tile, counts, weight):
    hbm = pl.BlockSpec(memory_space=pl.ANY)
    vmem = pl.BlockSpec(memory_space=pltpu.VMEM)
    smem = pl.BlockSpec(memory_space=pltpu.SMEM)
    dma = pltpu.SemaphoreType.DMA
    chunks = len(ROWS)

    def both(rows_a, rows_b, kind=BF16):
        return [pltpu.VMEM((A, *rows_a), kind), pltpu.VMEM((B, *rows_b), kind)]

    back_a, back_b, perm = pl.pallas_call(
        kernel,
        out_shape=(
            jax.ShapeDtypeStruct((A, D, 256), BF16),
            jax.ShapeDtypeStruct((B, D, 128), BF16),
            jax.ShapeDtypeStruct((2, LANES, 512), BF16),
        ),
        in_specs=[smem, vmem, vmem, hbm, hbm, hbm],
        out_specs=(hbm, hbm, hbm),
        scratch_shapes=[
            pltpu.VMEM((C, TILES * T), BF16),
            pltpu.VMEM((TILES, C, T), BF16),
            pltpu.VMEM((N, CAP, T, T), BF16),
            pltpu.VMEM((2, D, D), BF16),
            pltpu.VMEM((D, D), BF16),
            pltpu.VMEM((D, D), BF16),
            *both((N, CAP, 16, 128), (N, CAP // 2, 16, 128)),
            *both((N, CAP, 16, 128), (N, CAP // 2, 16, 128)),
            pltpu.VMEM((128, 128), F32),
            pltpu.VMEM((N, 1, 128), jnp.int32),
            pltpu.VMEM((N, 1, 128), jnp.int32),
            pltpu.VMEM((16 * 256, 128), F32),
            pltpu.VMEM((TILES * 16, 128), F32),
            *both((F, 128, 128), (F, 64, 128)),
            *both((F, 128, 128), (F, 64, 128)),
            pltpu.VMEM((F, C, SHARE), BF16),
            *both((D, 256), (D, 128)),
            *both((D, 256), (D, 128), F32),
            pltpu.VMEM((256, D), BF16),
            pltpu.VMEM((D, 256), F32),
            *both((D, 256), (D, 128)),
            pltpu.VMEM((2, LANES, 512), BF16),
            pltpu.VMEM((TILES, 256), BF16),
            dma,
            dma((N,)),
            dma,
            dma,
            dma,
            dma((chunks,)),
            dma,
            dma,
            dma,
            dma,
            dma((chunks,)),
            dma((chunks, N)),
            dma((chunks,)),
            dma((chunks,)),
            dma((chunks,)),
            dma((chunks,)),
        ],
        compiler_params=pltpu.CompilerParams(collective_id=1, has_side_effects=True, vmem_limit_bytes=60 * 2**20),
    )(src_tile.transpose(2, 0, 1), dst_tile.transpose(2, 0, 1), counts, features.T, tile_vals[0], weight)
    out = pl.pallas_call(
        place_kernel,
        grid=(4,),
        out_shape=jax.ShapeDtypeStruct((C, TILES * T), BF16),
        in_specs=[
            pl.BlockSpec((A, 256, 256), lambda i: (0, i, 0)),
            pl.BlockSpec((B, 256, 128), lambda i: (0, i, 0)),
            pl.BlockSpec((2, LANES, 512), lambda i: (0, 0, 0)),
        ],
        out_specs=pl.BlockSpec((C, 4 * SHARE), lambda i: (0, i)),
        compiler_params=pltpu.CompilerParams(vmem_limit_bytes=60 * 2**20),
    )(back_a, back_b, perm)
    return out.T


def solution(mesh):
    return jax.shard_map(
        on_device,
        mesh=mesh,
        in_specs=(
            P("nodes", "feat"),
            P("nodes", None, None, None, None),
            P("nodes", None, None),
            P("nodes", None, None),
            P("nodes", None),
            P(),
        ),
        out_specs=P("nodes", "feat"),
        check_vma=False,
    )
```

```python
import jax
import jax.numpy as jnp
from jax import lax
from jax.experimental import pallas as pl
from jax.experimental.pallas import tpu as pltpu
from jax.sharding import PartitionSpec as P

MESH = pl.DeviceIdType.MESH
BF16, F32 = jnp.bfloat16, jnp.float32
N = 16
F = 16
CAP = 12
T = 128
TILES = 128
C = 64
D = 1024
SHARE = 1024
ROWS = (16, 16, 16, 8, 8)
A, B = 3, 2
LOOK = 2
LANES = 128 * (A + B)
SCHEDULE = (
    ("sum", 0), ("layer", 0), ("sum", 1), ("layer", 1), ("sum", 2), ("sum", 3), ("layer", 2), ("layer", 3), ("sum", 4), ("layer", 4),
)

NT = (((1,), (1,)), ((), ()))

FAR = sorted(
    [(dy, dx) for dy in range(4) for dx in range(4) if (dy, dx) != (0, 0)],
    key=lambda o: -(min(o[0], 4 - o[0]) + min(o[1], 4 - o[1])),
)


def node_partner(n, step, sign):
    j = lax.div(step, 2)
    dz = 4 + (2 * lax.rem(j, 2) - 1) * lax.div(j + 1, 2)
    return lax.rem(lax.div(n, 2) + 8 + sign * dz, 8) * 2 + lax.rem(n + step + 1, 2)


def feat_partner(f, offset):
    dy, dx = offset
    return lax.rem(lax.div(f, 4) + dy, 4) * 4 + lax.rem(lax.rem(f, 4) + dx, 4)


def placing(tq):
    lane = lax.broadcasted_iota(jnp.int32, (LANES, 512), 0)
    row = lax.broadcasted_iota(jnp.int32, (LANES, 512), 1)
    tl, h, i = row // 128, (row // 64) % 2, row % 64
    by16 = (i // 16) * 128 + h * 64 + tl * 16 + i % 16
    by8 = A * 128 + ((i - 16 * A) // 8) * 128 + tq * 64 + h * 32 + tl * 8 + i % 8
    return (lane == jnp.where(i < 16 * A, by16, by8)).astype(F32).astype(BF16)


def kernel(
    src_ref,
    dst_ref,
    counts_ref,
    xt_ref,
    a_ref,
    w_ref,
    out_a,
    out_b,
    out_perm,
    xbuf,
    xtile,
    abuf,
    wbuf,
    wt0,
    wt1,
    zsend_a,
    zsend_b,
    zrecv_a,
    zrecv_b,
    turn,
    dmsg,
    dtgt,
    r32,
    g32,
    asend_a,
    asend_b,
    arecv_a,
    arecv_b,
    srecv,
    selfp_a,
    selfp_b,
    hs_a,
    hs_b,
    lhs,
    act,
    bsend_a,
    bsend_b,
    perm,
    onehot,
    xsem,
    asem,
    wsem,
    own_sem,
    perm_sem,
    back_sem,
    d_ss,
    d_rs,
    s_ss,
    s_rs,
    z_ss,
    z_rs,
    g_ss,
    g_rs,
    b_ss,
    b_rs,
):
    n, f = lax.axis_index("nodes"), lax.axis_index("feat")
    across = [feat_partner(f, o) for o in FAR]

    def node(i):
        return (i, f)

    def col(i):
        return (n, i)

    def to_node(step):
        return node_partner(n, step, 1)

    def from_node(step):
        return node_partner(n, step, -1)

    def part(a, b, k):
        return a.at[k] if k < A else b.at[k - A]

    x_copy = pltpu.make_async_copy(xt_ref, xbuf, xsem)
    x_copy.start()

    def a_copy(d):
        return pltpu.make_async_copy(a_ref.at[d], abuf.at[d], asem.at[d])

    @pl.loop(0, 16)
    def _(step):
        a_copy(to_node(step)).start()

    w_copy = pltpu.make_async_copy(w_ref, wbuf, wsem)
    w_copy.start()

    barrier = pltpu.get_barrier_semaphore()

    @pl.loop(0, 15)
    def _(step):
        pl.semaphore_signal(barrier, inc=1, device_id=node(to_node(step)), device_id_type=MESH)

    for to in across:
        pl.semaphore_signal(barrier, inc=1, device_id=col(to), device_id_type=MESH)

    x_copy.wait()

    @pl.loop(0, TILES, unroll=8)
    def _(t):
        xtile[t] = xbuf[:, pl.ds(pl.multiple_of(t * T, T), T)]

    def remote(src, dst, ss, rs, device):
        return pltpu.make_async_remote_copy(src, dst, ss, rs, device_id=device, device_id_type=MESH)

    def all_of(ref, size=1):
        return ref.at[pl.ds(0, 15 * size)]

    def d_send(to):
        return remote(dmsg.at[to], dtgt.at[n], d_ss, d_rs, node(to))

    def d_all():
        return remote(all_of(dmsg), all_of(dtgt), d_ss, d_rs, node(n))

    def share(i):
        return pl.ds(pl.multiple_of(i * SHARE, SHARE), SHARE)

    def s_send(to):
        return remote(xt_ref.at[:, share(to)], srecv.at[f], s_ss, s_rs, col(to))

    def s_all():
        return remote(all_of(srecv), all_of(srecv), s_ss, s_rs, col(f))

    def z_send(k, to):
        src, dst = part(zsend_a, zsend_b, k), part(zrecv_a, zrecv_b, k)
        return remote(src.at[to], dst.at[n], z_ss.at[k], z_rs.at[k, n], node(to))

    def z_recv(k, frm):
        src, dst = part(zsend_a, zsend_b, k), part(zrecv_a, zrecv_b, k)
        return remote(src.at[frm], dst.at[frm], z_ss.at[k], z_rs.at[k, frm], node(frm))

    def z_all(k):
        src, dst = part(zsend_a, zsend_b, k), part(zrecv_a, zrecv_b, k)
        return remote(all_of(src), all_of(dst), z_ss.at[k], z_rs.at[k, n], node(n))

    def g_send(k, to):
        src, dst = part(asend_a, asend_b, k), part(arecv_a, arecv_b, k)
        return remote(src.at[to], dst.at[f], g_ss.at[k], g_rs.at[k], col(to))

    def g_all(k):
        src, dst = part(asend_a, asend_b, k), part(arecv_a, arecv_b, k)
        return remote(all_of(src), all_of(dst), g_ss.at[k], g_rs.at[k], col(f))

    def rows(i):
        return pl.ds(pl.multiple_of(i * C, C), C)

    def b_send(k, to):
        src, dst = part(bsend_a, bsend_b, k), part(out_a, out_b, k)
        return remote(src.at[rows(to)], dst.at[rows(f)], b_ss.at[k], b_rs.at[k], col(to))

    def b_all(k):
        src, dst = part(bsend_a, bsend_b, k), part(out_a, out_b, k)
        return remote(all_of(src, C), all_of(dst, C), b_ss.at[k], b_rs.at[k], col(f))

    def b_own(k):
        src, dst = part(bsend_a, bsend_b, k), part(out_a, out_b, k)
        return pltpu.make_async_copy(src.at[rows(f)], dst.at[rows(f)], back_sem.at[k])

    none = jnp.zeros((C, T), BF16)

    def products(d, to_a, to_b, at):
        kept = None
        for c in range(CAP):
            a = abuf[d, c]
            left = jnp.concatenate([a[: T // 2], a[T // 2 :]], axis=1)
            x = xtile[src_ref[c, 0, d]]
            right = jnp.concatenate(
                [jnp.concatenate([x, none], axis=1), jnp.concatenate([none, x], axis=1)], axis=0
            )
            value = lax.dot_general(left, right, NT, preferred_element_type=F32)
            for k in range(A):
                to_a[k, at, c] = value[16 * k : 16 * k + 16].astype(BF16)
            if c % 2 == 0:
                kept = value
                continue
            for k in range(B):
                rows8 = slice(16 * A + 8 * k, 16 * A + 8 * k + 8)
                to_b[k, at, c // 2] = jnp.concatenate([kept[rows8], value[rows8]], axis=0).astype(BF16)

    def stage_one(step):
        d = to_node(step)
        a_copy(d).wait()
        products(d, zsend_a, zsend_b, d)

    stage_one(0)
    stage_one(1)
    pl.semaphore_wait(barrier, 30)
    for step in range(2):
        z_send(0, to_node(step)).start()

    for to in across:
        s_send(to).start()

    own_self = pltpu.make_async_copy(xt_ref.at[:, share(f)], srecv.at[f], own_sem)
    own_self.start()

    @pl.loop(2, 15)
    def _(step):
        stage_one(step)
        z_send(0, to_node(step)).start()

    turn[...] = jnp.zeros_like(turn)
    for c in range(CAP):
        used = jnp.where(counts_ref[...] > c, dst_ref[c] + 1, 0)
        turn[pl.ds(16 * (n % 8) + c, 1), 0:N] = used.astype(F32)
    turned = turn[...].T
    for d in range(N):
        dmsg[d] = turned[d : d + 1].astype(jnp.int32)

    @pl.loop(0, 15)
    def _(step):
        d_send(to_node(step)).start()

    for k in range(1, LOOK):

        @pl.loop(0, 15)
        def _(step):
            z_send(k, to_node(step)).start()

    a_copy(n).wait()
    products(n, zrecv_a, zrecv_b, n)

    dtgt[n] = dmsg[n]
    r32[...] = jnp.zeros_like(r32)
    perm[0] = placing(0)
    perm[1] = placing(1)
    perm_copy = pltpu.make_async_copy(perm, out_perm, perm_sem)
    perm_copy.start()
    w_copy.wait()

    for which, target in ((0, wt0), (1, wt1)):

        @pl.loop(0, 8)
        def _(i):
            at = pl.ds(pl.multiple_of(i * 128, 128), 128)
            for j in range(8):
                block = wbuf[which, at, 128 * j : 128 * j + 128]
                target[128 * j : 128 * j + 128, at] = block.T

    d_all().wait_recv()
    low, high = dtgt[0], dtgt[8]
    for s in range(1, 8):
        low, high = low + dtgt[s], high + dtgt[8 + s]
    wanted = jnp.concatenate([low, high], axis=1)
    place = lax.broadcasted_iota(jnp.int32, (TILES, 256), 0) + 1
    onehot[...] = (place == wanted).astype(F32).astype(BF16)

    def aggregate(k):
        nr = ROWS[k]
        got = part(zrecv_a, zrecv_b, k)

        def unpack(s):
            if nr == 16:
                for c in range(CAP):
                    r32[pl.ds(s * 16 + c, 16, stride=256), :] = got[s, c].astype(F32)
            else:
                for c in range(0, CAP, 2):
                    both = got[s, c // 2].astype(F32)
                    r32[pl.ds(s * 16 + c, 8, stride=256), :] = both[:8]
                    r32[pl.ds(s * 16 + c + 1, 8, stride=256), :] = both[8:]

        unpack(n)

        @pl.loop(0, 15)
        def _(step):
            s = from_node(step)
            z_recv(k, s).wait_recv()
            if k + LOOK < len(ROWS):
                z_send(k + LOOK, to_node(step)).start()
            unpack(s)

        @pl.loop(0, nr)
        def _(r):
            x = r32[pl.ds(pl.multiple_of(r * 256, 256), 256), :].astype(BF16)
            g32[pl.ds(r, TILES, stride=nr), :] = jnp.dot(onehot[...], x, preferred_element_type=F32)

        def packed(i):
            return g32[pl.ds(pl.multiple_of(i * 8 * nr, 8 * nr), 8 * nr), :].astype(BF16)

        out, mine = part(asend_a, asend_b, k), part(arecv_a, arecv_b, k)
        for to in across:
            out[to] = packed(to)
            g_send(k, to).start()
        mine[f] = packed(f)

    def self_part():
        own_self.wait()
        s_all().wait_recv()

        @pl.loop(0, 4)
        def _(i):
            at = pl.ds(pl.multiple_of(i * 256, 256), 256)
            by8 = [0.0] * B
            for tq in range(2):
                x = srecv[pl.ds(i * 4, 4), :, 512 * tq : 512 * tq + 512].reshape(256, 512)
                moved = lax.dot_general(x, perm[tq], NT, preferred_element_type=F32)
                for k in range(A):
                    selfp_a[k, at, 128 * tq : 128 * tq + 128] = moved[:, 128 * k : 128 * k + 128].astype(BF16)
                for k in range(B):
                    by8[k] = by8[k] + moved[:, 128 * (A + k) : 128 * (A + k) + 128]
            for k in range(B):
                selfp_b[k, at, :] = by8[k].astype(BF16)

        for k in range(A):
            hs_a[k] = jnp.dot(wt1[...], selfp_a[k], preferred_element_type=F32)
        for k in range(B):
            hs_b[k] = jnp.dot(wt1[...], selfp_b[k], preferred_element_type=F32)

    def layer(k):
        nr = ROWS[k]
        wide = 16 * nr
        g_all(k).wait_recv()
        got = part(arecv_a, arecv_b, k)
        lane = lax.broadcasted_iota(jnp.int32, (8 * nr, 128), 1)
        for m in range(8):
            a, b = got[2 * m].astype(F32), got[2 * m + 1].astype(F32)
            first = jnp.where(lane < 64, a, pltpu.roll(b, 64, 1)).astype(BF16)
            second = jnp.where(lane < 64, pltpu.roll(a, 64, 1), b).astype(BF16)
            cols = slice(128 * m, 128 * m + 128)
            for tq in range(2):
                at, of = 8 * nr * tq, slice(4 * nr * tq, 4 * nr * tq + 4 * nr)
                lhs[at : at + 4 * nr, cols] = first[of]
                lhs[at + 4 * nr : at + 8 * nr, cols] = second[of]

        here, away = part(hs_a, hs_b, k), part(bsend_a, bsend_b, k)
        hidden = here[...] + lax.dot_general(wt0[...], lhs[0:wide], NT, preferred_element_type=F32)
        act[:, 0:wide] = jnp.maximum(hidden, 0.0)
        total = jnp.sum(act[:, 0:wide] * act[:, 0:wide], axis=0, keepdims=True)
        away[...] = (act[:, 0:wide] * lax.rsqrt(total / D + 1e-06)).astype(BF16)
        for to in across:
            b_send(k, to).start()
        b_own(k).start()

    for step, k in SCHEDULE:
        if step == "sum":
            aggregate(k)
        else:
            if k == 0:
                self_part()
            layer(k)

    perm_copy.wait()
    d_all().wait_send()
    s_all().wait_send()
    for k in range(len(ROWS)):
        z_all(k).wait_send()
        g_all(k).wait_send()
        b_all(k).wait_send()
        b_own(k).wait()
        b_all(k).wait_recv()


def place_kernel(a_ref, b_ref, perm_ref, out_ref, abuf, bbuf, pbuf, obuf, a_sem, b_sem, p_sem, o_sem):
    def fetch(i):
        at = pl.ds(256 * i, 256)
        return (
            pltpu.make_async_copy(a_ref.at[:, at], abuf.at[i], a_sem.at[i]),
            pltpu.make_async_copy(b_ref.at[:, at], bbuf.at[i], b_sem.at[i]),
        )

    def fetch_perm(tq):
        return pltpu.make_async_copy(perm_ref.at[tq], pbuf.at[tq], p_sem.at[tq])

    def store(i):
        return pltpu.make_async_copy(obuf.at[i], out_ref.at[:, pl.ds(4 * SHARE * i, 4 * SHARE)], o_sem.at[i])

    fetch_perm(0).start()
    for i in range(4):
        for copy in fetch(i):
            copy.start()
        if i == 0:
            fetch_perm(1).start()
    for i in range(4):
        for tq in range(2):
            if i == 0:
                fetch_perm(tq).wait()
            if tq == 0:
                for copy in fetch(i):
                    copy.wait()
            x = [abuf[i, k, :, 128 * tq : 128 * tq + 128] for k in range(A)] + [bbuf[i, k] for k in range(B)]
            moved = jnp.dot(jnp.concatenate(x, axis=1), pbuf[tq], preferred_element_type=F32).astype(BF16)
            for j in range(4):
                obuf[i, :, SHARE * j + 512 * tq : SHARE * j + 512 * tq + 512] = moved[C * j : C * j + C]
        store(i).start()
    for i in range(4):
        store(i).wait()


def on_device(features, tile_vals, src_tile, dst_tile, counts, weight):
    hbm = pl.BlockSpec(memory_space=pl.ANY)
    vmem = pl.BlockSpec(memory_space=pltpu.VMEM)
    smem = pl.BlockSpec(memory_space=pltpu.SMEM)
    dma = pltpu.SemaphoreType.DMA
    chunks = len(ROWS)

    def both(rows_a, rows_b, kind=BF16):
        return [pltpu.VMEM((A, *rows_a), kind), pltpu.VMEM((B, *rows_b), kind)]

    back_a, back_b, perm = pl.pallas_call(
        kernel,
        out_shape=(
            jax.ShapeDtypeStruct((A, D, 256), BF16),
            jax.ShapeDtypeStruct((B, D, 128), BF16),
            jax.ShapeDtypeStruct((2, LANES, 512), BF16),
        ),
        in_specs=[smem, vmem, vmem, hbm, hbm, hbm],
        out_specs=(hbm, hbm, hbm),
        scratch_shapes=[
            pltpu.VMEM((C, TILES * T), BF16),
            pltpu.VMEM((TILES, C, T), BF16),
            pltpu.VMEM((N, CAP, T, T), BF16),
            pltpu.VMEM((2, D, D), BF16),
            pltpu.VMEM((D, D), BF16),
            pltpu.VMEM((D, D), BF16),
            *both((N, CAP, 16, 128), (N, CAP // 2, 16, 128)),
            *both((N, CAP, 16, 128), (N, CAP // 2, 16, 128)),
            pltpu.VMEM((128, 128), F32),
            pltpu.VMEM((N, 1, 128), jnp.int32),
            pltpu.VMEM((N, 1, 128), jnp.int32),
            pltpu.VMEM((16 * 256, 128), F32),
            pltpu.VMEM((TILES * 16, 128), F32),
            *both((F, 128, 128), (F, 64, 128)),
            *both((F, 128, 128), (F, 64, 128)),
            pltpu.VMEM((F, C, SHARE), BF16),
            *both((D, 256), (D, 128)),
            *both((D, 256), (D, 128), F32),
            pltpu.VMEM((256, D), BF16),
            pltpu.VMEM((D, 256), F32),
            *both((D, 256), (D, 128)),
            pltpu.VMEM((2, LANES, 512), BF16),
            pltpu.VMEM((TILES, 256), BF16),
            dma,
            dma((N,)),
            dma,
            dma,
            dma,
            dma((chunks,)),
            dma,
            dma,
            dma,
            dma,
            dma((chunks,)),
            dma((chunks, N)),
            dma((chunks,)),
            dma((chunks,)),
            dma((chunks,)),
            dma((chunks,)),
        ],
        compiler_params=pltpu.CompilerParams(collective_id=1, has_side_effects=True, vmem_limit_bytes=60 * 2**20),
    )(src_tile.transpose(2, 0, 1), dst_tile.transpose(2, 0, 1), counts, features.T, tile_vals[0], weight)
    out = pl.pallas_call(
        place_kernel,
        out_shape=jax.ShapeDtypeStruct((C, TILES * T), BF16),
        in_specs=[hbm, hbm, hbm],
        out_specs=hbm,
        scratch_shapes=[
            pltpu.VMEM((4, A, 256, 256), BF16),
            pltpu.VMEM((4, B, 256, 128), BF16),
            pltpu.VMEM((2, LANES, 512), BF16),
            pltpu.VMEM((4, C, 4 * SHARE), BF16),
            dma((4,)),
            dma((4,)),
            dma((2,)),
            dma((4,)),
        ],
        compiler_params=pltpu.CompilerParams(vmem_limit_bytes=60 * 2**20),
    )(back_a, back_b, perm)
    return out.T


def solution(mesh):
    return jax.shard_map(
        on_device,
        mesh=mesh,
        in_specs=(
            P("nodes", "feat"),
            P("nodes", None, None, None, None),
            P("nodes", None, None),
            P("nodes", None, None),
            P("nodes", None),
            P(),
        ),
        out_specs=P("nodes", "feat"),
        check_vma=False,
    )
```

```python
import jax
import jax.numpy as jnp
from jax import lax
from jax.experimental import pallas as pl
from jax.experimental.pallas import tpu as pltpu
from jax.sharding import PartitionSpec as P

MESH = pl.DeviceIdType.MESH
BF16, F32 = jnp.bfloat16, jnp.float32
N = 16
F = 16
CAP = 12
T = 128
TILES = 128
C = 64
D = 1024
SHARE = 1024
ROWS = (16, 16, 16, 8, 8)
A, B = 3, 2
LOOK = 2
LANES = 128 * (A + B)
SCHEDULE = (
    ("sum", 0), ("layer", 0), ("sum", 1), ("layer", 1), ("sum", 2), ("sum", 3), ("layer", 2), ("layer", 3), ("sum", 4), ("layer", 4),
)

NT = (((1,), (1,)), ((), ()))

FAR = sorted(
    [(dy, dx) for dy in range(4) for dx in range(4) if (dy, dx) != (0, 0)],
    key=lambda o: -(min(o[0], 4 - o[0]) + min(o[1], 4 - o[1])),
)


def node_partner(n, step, sign):
    j = lax.div(step, 2)
    dz = 4 + (2 * lax.rem(j, 2) - 1) * lax.div(j + 1, 2)
    return lax.rem(lax.div(n, 2) + 8 + sign * dz, 8) * 2 + lax.rem(n + step + 1, 2)


def feat_partner(f, offset):
    dy, dx = offset
    return lax.rem(lax.div(f, 4) + dy, 4) * 4 + lax.rem(lax.rem(f, 4) + dx, 4)


def placing(tq):
    lane = lax.broadcasted_iota(jnp.int32, (LANES, 512), 0)
    row = lax.broadcasted_iota(jnp.int32, (LANES, 512), 1)
    tl, h, i = row // 128, (row // 64) % 2, row % 64
    by16 = (i // 16) * 128 + h * 64 + tl * 16 + i % 16
    by8 = A * 128 + ((i - 16 * A) // 8) * 128 + tq * 64 + h * 32 + tl * 8 + i % 8
    return (lane == jnp.where(i < 16 * A, by16, by8)).astype(F32).astype(BF16)


def kernel(
    src_ref,
    dst_ref,
    counts_ref,
    xt_ref,
    a_ref,
    w_ref,
    out_a,
    out_b,
    out_perm,
    xbuf,
    xtile,
    abuf,
    wbuf,
    wt0,
    wt1,
    zsend_a,
    zsend_b,
    zrecv_a,
    zrecv_b,
    turn,
    dmsg,
    dtgt,
    r32,
    g32,
    asend_a,
    asend_b,
    arecv_a,
    arecv_b,
    srecv,
    selfp_a,
    selfp_b,
    hs_a,
    hs_b,
    lhs,
    act,
    bsend_a,
    bsend_b,
    perm,
    onehot,
    xsem,
    asem,
    wsem,
    own_sem,
    perm_sem,
    back_sem,
    d_ss,
    d_rs,
    s_ss,
    s_rs,
    z_ss,
    z_rs,
    g_ss,
    g_rs,
    b_ss,
    b_rs,
):
    n, f = lax.axis_index("nodes"), lax.axis_index("feat")
    across = [feat_partner(f, o) for o in FAR]

    def node(i):
        return (i, f)

    def col(i):
        return (n, i)

    def to_node(step):
        return node_partner(n, step, 1)

    def from_node(step):
        return node_partner(n, step, -1)

    def part(a, b, k):
        return a.at[k] if k < A else b.at[k - A]

    x_copy = pltpu.make_async_copy(xt_ref, xbuf, xsem)
    x_copy.start()

    def a_copy(d):
        return pltpu.make_async_copy(a_ref.at[d], abuf.at[d], asem.at[d])

    @pl.loop(0, 16)
    def _(step):
        a_copy(to_node(step)).start()

    w_copy = pltpu.make_async_copy(w_ref, wbuf, wsem)
    w_copy.start()

    barrier = pltpu.get_barrier_semaphore()

    @pl.loop(0, 15)
    def _(step):
        pl.semaphore_signal(barrier, inc=1, device_id=node(to_node(step)), device_id_type=MESH)

    for to in across:
        pl.semaphore_signal(barrier, inc=1, device_id=col(to), device_id_type=MESH)

    x_copy.wait()

    @pl.loop(0, TILES, unroll=8)
    def _(t):
        xtile[t] = xbuf[:, pl.ds(pl.multiple_of(t * T, T), T)]

    def remote(src, dst, ss, rs, device):
        return pltpu.make_async_remote_copy(src, dst, ss, rs, device_id=device, device_id_type=MESH)

    def all_of(ref, size=1):
        return ref.at[pl.ds(0, 15 * size)]

    def d_send(to):
        return remote(dmsg.at[to], dtgt.at[n], d_ss, d_rs, node(to))

    def d_all():
        return remote(all_of(dmsg), all_of(dtgt), d_ss, d_rs, node(n))

    def share(i):
        return pl.ds(pl.multiple_of(i * SHARE, SHARE), SHARE)

    def s_send(to):
        return remote(xt_ref.at[:, share(to)], srecv.at[f], s_ss, s_rs, col(to))

    def s_all():
        return remote(all_of(srecv), all_of(srecv), s_ss, s_rs, col(f))

    def z_send(k, to):
        src, dst = part(zsend_a, zsend_b, k), part(zrecv_a, zrecv_b, k)
        return remote(src.at[to], dst.at[n], z_ss.at[k], z_rs.at[k, n], node(to))

    def z_recv(k, frm):
        src, dst = part(zsend_a, zsend_b, k), part(zrecv_a, zrecv_b, k)
        return remote(src.at[frm], dst.at[frm], z_ss.at[k], z_rs.at[k, frm], node(frm))

    def z_all(k):
        src, dst = part(zsend_a, zsend_b, k), part(zrecv_a, zrecv_b, k)
        return remote(all_of(src), all_of(dst), z_ss.at[k], z_rs.at[k, n], node(n))

    def g_send(k, to):
        src, dst = part(asend_a, asend_b, k), part(arecv_a, arecv_b, k)
        return remote(src.at[to], dst.at[f], g_ss.at[k], g_rs.at[k], col(to))

    def g_all(k):
        src, dst = part(asend_a, asend_b, k), part(arecv_a, arecv_b, k)
        return remote(all_of(src), all_of(dst), g_ss.at[k], g_rs.at[k], col(f))

    def rows(i):
        return pl.ds(pl.multiple_of(i * C, C), C)

    def b_send(k, to):
        src, dst = part(bsend_a, bsend_b, k), part(out_a, out_b, k)
        return remote(src.at[rows(to)], dst.at[rows(f)], b_ss.at[k], b_rs.at[k], col(to))

    def b_all(k):
        src, dst = part(bsend_a, bsend_b, k), part(out_a, out_b, k)
        return remote(all_of(src, C), all_of(dst, C), b_ss.at[k], b_rs.at[k], col(f))

    def b_own(k):
        src, dst = part(bsend_a, bsend_b, k), part(out_a, out_b, k)
        return pltpu.make_async_copy(src.at[rows(f)], dst.at[rows(f)], back_sem.at[k])

    none = jnp.zeros((C, T), BF16)

    def products(d, to_a, to_b, at):
        kept = None
        for c in range(CAP):
            a = abuf[d, c]
            left = jnp.concatenate([a[: T // 2], a[T // 2 :]], axis=1)
            x = xtile[src_ref[c, 0, d]]
            right = jnp.concatenate(
                [jnp.concatenate([x, none], axis=1), jnp.concatenate([none, x], axis=1)], axis=0
            )
            value = lax.dot_general(left, right, NT, preferred_element_type=F32)
            for k in range(A):
                to_a[k, at, c] = value[16 * k : 16 * k + 16].astype(BF16)
            if c % 2 == 0:
                kept = value
                continue
            for k in range(B):
                rows8 = slice(16 * A + 8 * k, 16 * A + 8 * k + 8)
                to_b[k, at, c // 2] = jnp.concatenate([kept[rows8], value[rows8]], axis=0).astype(BF16)

    def stage_one(step):
        d = to_node(step)
        a_copy(d).wait()
        products(d, zsend_a, zsend_b, d)

    stage_one(0)
    pl.semaphore_wait(barrier, 30)
    z_send(0, to_node(0)).start()

    for to in across:
        s_send(to).start()

    own_self = pltpu.make_async_copy(xt_ref.at[:, share(f)], srecv.at[f], own_sem)
    own_self.start()

    @pl.loop(1, 15)
    def _(step):
        stage_one(step)
        z_send(0, to_node(step)).start()

    turn[...] = jnp.zeros_like(turn)
    for c in range(CAP):
        used = jnp.where(counts_ref[...] > c, dst_ref[c] + 1, 0)
        turn[pl.ds(16 * (n % 8) + c, 1), 0:N] = used.astype(F32)
    turned = turn[...].T
    for d in range(N):
        dmsg[d] = turned[d : d + 1].astype(jnp.int32)

    @pl.loop(0, 15)
    def _(step):
        d_send(to_node(step)).start()

    for k in range(1, LOOK):

        @pl.loop(0, 15)
        def _(step):
            z_send(k, to_node(step)).start()

    a_copy(n).wait()
    products(n, zrecv_a, zrecv_b, n)

    dtgt[n] = dmsg[n]
    r32[...] = jnp.zeros_like(r32)
    perm[0] = placing(0)
    perm[1] = placing(1)
    perm_copy = pltpu.make_async_copy(perm, out_perm, perm_sem)
    perm_copy.start()
    w_copy.wait()

    for which, target in ((0, wt0), (1, wt1)):

        @pl.loop(0, 8)
        def _(i):
            at = pl.ds(pl.multiple_of(i * 128, 128), 128)
            for j in range(8):
                block = wbuf[which, at, 128 * j : 128 * j + 128]
                target[128 * j : 128 * j + 128, at] = block.T

    d_all().wait_recv()
    low, high = dtgt[0], dtgt[8]
    for s in range(1, 8):
        low, high = low + dtgt[s], high + dtgt[8 + s]
    wanted = jnp.concatenate([low, high], axis=1)
    place = lax.broadcasted_iota(jnp.int32, (TILES, 256), 0) + 1
    onehot[...] = (place == wanted).astype(F32).astype(BF16)

    def aggregate(k):
        nr = ROWS[k]
        got = part(zrecv_a, zrecv_b, k)

        def unpack(s):
            if nr == 16:
                for c in range(CAP):
                    r32[pl.ds(s * 16 + c, 16, stride=256), :] = got[s, c].astype(F32)
            else:
                for c in range(0, CAP, 2):
                    both = got[s, c // 2].astype(F32)
                    r32[pl.ds(s * 16 + c, 8, stride=256), :] = both[:8]
                    r32[pl.ds(s * 16 + c + 1, 8, stride=256), :] = both[8:]

        unpack(n)

        @pl.loop(0, 15)
        def _(step):
            s = from_node(step)
            z_recv(k, s).wait_recv()
            if k + LOOK < len(ROWS):
                z_send(k + LOOK, to_node(step)).start()
            unpack(s)

        def rows_of(r):
            return r32[pl.ds(pl.multiple_of(r * 256, 256), 256), :]

        @pl.loop(0, nr // 4)
        def _(quarter):
            for pair in range(2):
                r = quarter * 4 + 2 * pair
                x = jnp.concatenate([rows_of(r), rows_of(r + 1)], axis=1).astype(BF16)
                sums = jnp.dot(onehot[...], x, preferred_element_type=F32)
                g32[pl.ds(r, TILES, stride=nr), :] = sums[:, :128]
                g32[pl.ds(r + 1, TILES, stride=nr), :] = sums[:, 128:]

        def packed(i):
            return g32[pl.ds(pl.multiple_of(i * 8 * nr, 8 * nr), 8 * nr), :].astype(BF16)

        out, mine = part(asend_a, asend_b, k), part(arecv_a, arecv_b, k)
        for to in across:
            out[to] = packed(to)
            g_send(k, to).start()
        mine[f] = packed(f)

    def self_part():
        own_self.wait()
        s_all().wait_recv()

        @pl.loop(0, 4)
        def _(i):
            at = pl.ds(pl.multiple_of(i * 256, 256), 256)
            by8 = [0.0] * B
            for tq in range(2):
                x = srecv[pl.ds(i * 4, 4), :, 512 * tq : 512 * tq + 512].reshape(256, 512)
                moved = lax.dot_general(x, perm[tq], NT, preferred_element_type=F32)
                for k in range(A):
                    selfp_a[k, at, 128 * tq : 128 * tq + 128] = moved[:, 128 * k : 128 * k + 128].astype(BF16)
                for k in range(B):
                    by8[k] = by8[k] + moved[:, 128 * (A + k) : 128 * (A + k) + 128]
            for k in range(B):
                selfp_b[k, at, :] = by8[k].astype(BF16)

        for k in range(A):
            hs_a[k] = jnp.dot(wt1[...], selfp_a[k], preferred_element_type=F32)
        for k in range(B):
            hs_b[k] = jnp.dot(wt1[...], selfp_b[k], preferred_element_type=F32)

    def layer(k):
        nr = ROWS[k]
        wide = 16 * nr
        g_all(k).wait_recv()
        got = part(arecv_a, arecv_b, k)
        lane = lax.broadcasted_iota(jnp.int32, (8 * nr, 128), 1)
        for m in range(8):
            a, b = got[2 * m].astype(F32), got[2 * m + 1].astype(F32)
            first = jnp.where(lane < 64, a, pltpu.roll(b, 64, 1)).astype(BF16)
            second = jnp.where(lane < 64, pltpu.roll(a, 64, 1), b).astype(BF16)
            cols = slice(128 * m, 128 * m + 128)
            for tq in range(2):
                at, of = 8 * nr * tq, slice(4 * nr * tq, 4 * nr * tq + 4 * nr)
                lhs[at : at + 4 * nr, cols] = first[of]
                lhs[at + 4 * nr : at + 8 * nr, cols] = second[of]

        here, away = part(hs_a, hs_b, k), part(bsend_a, bsend_b, k)
        total = jnp.zeros((1, wide), F32)
        for at in range(0, D, D // 2):
            half = slice(at, at + D // 2)
            hidden = here[half] + lax.dot_general(wt0[half], lhs[0:wide], NT, preferred_element_type=F32)
            active = jnp.maximum(hidden, 0.0)
            act[half, 0:wide] = active
            total = total + jnp.sum(active * active, axis=0, keepdims=True)
        away[...] = (act[:, 0:wide] * lax.rsqrt(total / D + 1e-06)).astype(BF16)
        for to in across:
            b_send(k, to).start()
        b_own(k).start()

    for step, k in SCHEDULE:
        if step == "sum":
            aggregate(k)
        else:
            if k == 0:
                self_part()
            layer(k)

    perm_copy.wait()
    d_all().wait_send()
    s_all().wait_send()
    for k in range(len(ROWS)):
        z_all(k).wait_send()
        g_all(k).wait_send()
        b_all(k).wait_send()
        b_own(k).wait()
        b_all(k).wait_recv()


def place_kernel(a_ref, b_ref, perm_ref, out_ref, abuf, bbuf, pbuf, obuf, a_sem, b_sem, p_sem, o_sem):
    def fetch(i):
        at = pl.ds(256 * i, 256)
        return (
            pltpu.make_async_copy(a_ref.at[:, at], abuf.at[i], a_sem.at[i]),
            pltpu.make_async_copy(b_ref.at[:, at], bbuf.at[i], b_sem.at[i]),
        )

    def fetch_perm(tq):
        return pltpu.make_async_copy(perm_ref.at[tq], pbuf.at[tq], p_sem.at[tq])

    def store(i):
        return pltpu.make_async_copy(obuf.at[i], out_ref.at[:, pl.ds(4 * SHARE * i, 4 * SHARE)], o_sem.at[i])

    fetch_perm(0).start()
    for i in range(4):
        for copy in fetch(i):
            copy.start()
        if i == 0:
            fetch_perm(1).start()
    for i in range(4):
        for tq in range(2):
            if i == 0:
                fetch_perm(tq).wait()
            if tq == 0:
                for copy in fetch(i):
                    copy.wait()
            x = [abuf[i, k, :, 128 * tq : 128 * tq + 128] for k in range(A)] + [bbuf[i, k] for k in range(B)]
            moved = jnp.dot(jnp.concatenate(x, axis=1), pbuf[tq], preferred_element_type=F32).astype(BF16)
            for j in range(4):
                obuf[i, :, SHARE * j + 512 * tq : SHARE * j + 512 * tq + 512] = moved[C * j : C * j + C]
        store(i).start()
    for i in range(4):
        store(i).wait()


def on_device(features, tile_vals, src_tile, dst_tile, counts, weight):
    hbm = pl.BlockSpec(memory_space=pl.ANY)
    vmem = pl.BlockSpec(memory_space=pltpu.VMEM)
    smem = pl.BlockSpec(memory_space=pltpu.SMEM)
    dma = pltpu.SemaphoreType.DMA
    chunks = len(ROWS)

    def both(rows_a, rows_b, kind=BF16):
        return [pltpu.VMEM((A, *rows_a), kind), pltpu.VMEM((B, *rows_b), kind)]

    back_a, back_b, perm = pl.pallas_call(
        kernel,
        out_shape=(
            jax.ShapeDtypeStruct((A, D, 256), BF16),
            jax.ShapeDtypeStruct((B, D, 128), BF16),
            jax.ShapeDtypeStruct((2, LANES, 512), BF16),
        ),
        in_specs=[smem, vmem, vmem, hbm, hbm, hbm],
        out_specs=(hbm, hbm, hbm),
        scratch_shapes=[
            pltpu.VMEM((C, TILES * T), BF16),
            pltpu.VMEM((TILES, C, T), BF16),
            pltpu.VMEM((N, CAP, T, T), BF16),
            pltpu.VMEM((2, D, D), BF16),
            pltpu.VMEM((D, D), BF16),
            pltpu.VMEM((D, D), BF16),
            *both((N, CAP, 16, 128), (N, CAP // 2, 16, 128)),
            *both((N, CAP, 16, 128), (N, CAP // 2, 16, 128)),
            pltpu.VMEM((128, 128), F32),
            pltpu.VMEM((N, 1, 128), jnp.int32),
            pltpu.VMEM((N, 1, 128), jnp.int32),
            pltpu.VMEM((16 * 256, 128), F32),
            pltpu.VMEM((TILES * 16, 128), F32),
            *both((F, 128, 128), (F, 64, 128)),
            *both((F, 128, 128), (F, 64, 128)),
            pltpu.VMEM((F, C, SHARE), BF16),
            *both((D, 256), (D, 128)),
            *both((D, 256), (D, 128), F32),
            pltpu.VMEM((256, D), BF16),
            pltpu.VMEM((D, 256), F32),
            *both((D, 256), (D, 128)),
            pltpu.VMEM((2, LANES, 512), BF16),
            pltpu.VMEM((TILES, 256), BF16),
            dma,
            dma((N,)),
            dma,
            dma,
            dma,
            dma((chunks,)),
            dma,
            dma,
            dma,
            dma,
            dma((chunks,)),
            dma((chunks, N)),
            dma((chunks,)),
            dma((chunks,)),
            dma((chunks,)),
            dma((chunks,)),
        ],
        compiler_params=pltpu.CompilerParams(collective_id=1, has_side_effects=True, vmem_limit_bytes=60 * 2**20),
    )(src_tile.transpose(2, 0, 1), dst_tile.transpose(2, 0, 1), counts, features.T, tile_vals[0], weight)
    out = pl.pallas_call(
        place_kernel,
        out_shape=jax.ShapeDtypeStruct((C, TILES * T), BF16),
        in_specs=[hbm, hbm, hbm],
        out_specs=hbm,
        scratch_shapes=[
            pltpu.VMEM((4, A, 256, 256), BF16),
            pltpu.VMEM((4, B, 256, 128), BF16),
            pltpu.VMEM((2, LANES, 512), BF16),
            pltpu.VMEM((4, C, 4 * SHARE), BF16),
            dma((4,)),
            dma((4,)),
            dma((2,)),
            dma((4,)),
        ],
        compiler_params=pltpu.CompilerParams(vmem_limit_bytes=60 * 2**20),
    )(back_a, back_b, perm)
    return out.T


def solution(mesh):
    return jax.shard_map(
        on_device,
        mesh=mesh,
        in_specs=(
            P("nodes", "feat"),
            P("nodes", None, None, None, None),
            P("nodes", None, None),
            P("nodes", None, None),
            P("nodes", None),
            P(),
        ),
        out_specs=P("nodes", "feat"),
        check_vma=False,
    )
```

```python
import jax
import jax.numpy as jnp
from jax import lax
from jax.experimental import pallas as pl
from jax.experimental.pallas import tpu as pltpu
from jax.sharding import PartitionSpec as P

MESH = pl.DeviceIdType.MESH
BF16, F32 = jnp.bfloat16, jnp.float32
N = 16
F = 16
CAP = 12
T = 128
TILES = 128
C = 64
D = 1024
SHARE = 1024
ROWS = (16, 16, 16, 8, 8)
A, B = 3, 2
LOOK = 2
LAST = len(ROWS) - 1
LANES = 128 * (A + B)
MOST = 128 * LAST
SCHEDULE = (
    ("sum", 0), ("layer", 0), ("sum", 1), ("layer", 1), ("sum", 2), ("sum", 3), ("layer", 2), ("layer", 3), ("sum", 4), ("layer", 4),
)

NT = (((1,), (1,)), ((), ()))

FAR = sorted(
    [(dy, dx) for dy in range(4) for dx in range(4) if (dy, dx) != (0, 0)],
    key=lambda o: -(min(o[0], 4 - o[0]) + min(o[1], 4 - o[1])),
)


def node_partner(n, step, sign):
    j = lax.div(step, 2)
    dz = 4 + (2 * lax.rem(j, 2) - 1) * lax.div(j + 1, 2)
    return lax.rem(lax.div(n, 2) + 8 + sign * dz, 8) * 2 + lax.rem(n + step + 1, 2)


def feat_partner(f, offset):
    dy, dx = offset
    return lax.rem(lax.div(f, 4) + dy, 4) * 4 + lax.rem(lax.rem(f, 4) + dx, 4)


def placing(tq):
    lane = lax.broadcasted_iota(jnp.int32, (LANES, 512), 0)
    row = lax.broadcasted_iota(jnp.int32, (LANES, 512), 1)
    tl, h, i = row // 128, (row // 64) % 2, row % 64
    by16 = (i // 16) * 128 + h * 64 + tl * 16 + i % 16
    by8 = A * 128 + ((i - 16 * A) // 8) * 128 + tq * 64 + h * 32 + tl * 8 + i % 8
    return (lane == jnp.where(i < 16 * A, by16, by8)).astype(F32).astype(BF16)


def kernel(
    src_ref,
    dst_ref,
    counts_ref,
    xt_ref,
    a_ref,
    w_ref,
    out_most,
    out_last,
    out_perm,
    xbuf,
    xtile,
    abuf,
    wbuf,
    wt0,
    wt1,
    zsend_a,
    zsend_b,
    zrecv_a,
    zrecv_b,
    turn,
    dmsg,
    dtgt,
    r32,
    g32,
    asend_a,
    asend_b,
    arecv_a,
    arecv_b,
    srecv,
    selfp_a,
    selfp_b,
    hs_a,
    hs_b,
    lhs,
    act,
    bsend_a,
    bsend_b,
    brecv_a,
    brecv_b,
    most,
    perm,
    onehot,
    xsem,
    asem,
    wsem,
    own_sem,
    perm_sem,
    most_sem,
    back_sem,
    d_ss,
    d_rs,
    s_ss,
    s_rs,
    z_ss,
    z_rs,
    g_ss,
    g_rs,
    b_ss,
    b_rs,
):
    n, f = lax.axis_index("nodes"), lax.axis_index("feat")
    across = [feat_partner(f, o) for o in FAR]

    def node(i):
        return (i, f)

    def col(i):
        return (n, i)

    def to_node(step):
        return node_partner(n, step, 1)

    def from_node(step):
        return node_partner(n, step, -1)

    def part(a, b, k):
        return a.at[k] if k < A else b.at[k - A]

    def back(k):
        return out_last if k == LAST else part(brecv_a, brecv_b, k)

    x_copy = pltpu.make_async_copy(xt_ref, xbuf, xsem)
    x_copy.start()

    def a_copy(d):
        return pltpu.make_async_copy(a_ref.at[d], abuf.at[d], asem.at[d])

    @pl.loop(0, 16)
    def _(step):
        a_copy(to_node(step)).start()

    w_copy = pltpu.make_async_copy(w_ref, wbuf, wsem)
    w_copy.start()

    barrier = pltpu.get_barrier_semaphore()

    @pl.loop(0, 15)
    def _(step):
        pl.semaphore_signal(barrier, inc=1, device_id=node(to_node(step)), device_id_type=MESH)

    for to in across:
        pl.semaphore_signal(barrier, inc=1, device_id=col(to), device_id_type=MESH)

    x_copy.wait()

    @pl.loop(0, TILES, unroll=8)
    def _(t):
        xtile[t] = xbuf[:, pl.ds(pl.multiple_of(t * T, T), T)]

    def remote(src, dst, ss, rs, device):
        return pltpu.make_async_remote_copy(src, dst, ss, rs, device_id=device, device_id_type=MESH)

    def all_of(ref, size=1):
        return ref.at[pl.ds(0, 15 * size)]

    def d_send(to):
        return remote(dmsg.at[to], dtgt.at[n], d_ss, d_rs, node(to))

    def d_all():
        return remote(all_of(dmsg), all_of(dtgt), d_ss, d_rs, node(n))

    def share(i):
        return pl.ds(pl.multiple_of(i * SHARE, SHARE), SHARE)

    def s_send(to):
        return remote(xt_ref.at[:, share(to)], srecv.at[f], s_ss, s_rs, col(to))

    def s_all():
        return remote(all_of(srecv), all_of(srecv), s_ss, s_rs, col(f))

    def z_send(k, to):
        src, dst = part(zsend_a, zsend_b, k), part(zrecv_a, zrecv_b, k)
        return remote(src.at[to], dst.at[n], z_ss.at[k], z_rs.at[k, n], node(to))

    def z_recv(k, frm):
        src, dst = part(zsend_a, zsend_b, k), part(zrecv_a, zrecv_b, k)
        return remote(src.at[frm], dst.at[frm], z_ss.at[k], z_rs.at[k, frm], node(frm))

    def z_all(k):
        src, dst = part(zsend_a, zsend_b, k), part(zrecv_a, zrecv_b, k)
        return remote(all_of(src), all_of(dst), z_ss.at[k], z_rs.at[k, n], node(n))

    def g_send(k, to):
        src, dst = part(asend_a, asend_b, k), part(arecv_a, arecv_b, k)
        return remote(src.at[to], dst.at[f], g_ss.at[k], g_rs.at[k], col(to))

    def g_all(k):
        src, dst = part(asend_a, asend_b, k), part(arecv_a, arecv_b, k)
        return remote(all_of(src), all_of(dst), g_ss.at[k], g_rs.at[k], col(f))

    def rows(i):
        return pl.ds(pl.multiple_of(i * C, C), C)

    def b_send(k, to):
        src, dst = part(bsend_a, bsend_b, k), back(k)
        return remote(src.at[rows(to)], dst.at[rows(f)], b_ss.at[k], b_rs.at[k], col(to))

    def b_all(k):
        src, dst = part(bsend_a, bsend_b, k), back(k)
        return remote(all_of(src, C), all_of(dst, C), b_ss.at[k], b_rs.at[k], col(f))

    def b_own(k):
        src, dst = part(bsend_a, bsend_b, k), back(k)
        return pltpu.make_async_copy(src.at[rows(f)], dst.at[rows(f)], back_sem.at[k])

    none = jnp.zeros((C, T), BF16)

    def products(d, to_a, to_b, at):
        kept = None
        for c in range(CAP):
            a = abuf[d, c]
            left = jnp.concatenate([a[: T // 2], a[T // 2 :]], axis=1)
            x = xtile[src_ref[c, 0, d]]
            right = jnp.concatenate(
                [jnp.concatenate([x, none], axis=1), jnp.concatenate([none, x], axis=1)], axis=0
            )
            value = lax.dot_general(left, right, NT, preferred_element_type=F32)
            for k in range(A):
                to_a[k, at, c] = value[16 * k : 16 * k + 16].astype(BF16)
            if c % 2 == 0:
                kept = value
                continue
            for k in range(B):
                rows8 = slice(16 * A + 8 * k, 16 * A + 8 * k + 8)
                to_b[k, at, c // 2] = jnp.concatenate([kept[rows8], value[rows8]], axis=0).astype(BF16)

    def stage_one(step):
        d = to_node(step)
        a_copy(d).wait()
        products(d, zsend_a, zsend_b, d)

    stage_one(0)
    pl.semaphore_wait(barrier, 30)
    z_send(0, to_node(0)).start()

    for to in across:
        s_send(to).start()

    own_self = pltpu.make_async_copy(xt_ref.at[:, share(f)], srecv.at[f], own_sem)
    own_self.start()

    @pl.loop(1, 15)
    def _(step):
        stage_one(step)
        z_send(0, to_node(step)).start()

    turn[...] = jnp.zeros_like(turn)
    for c in range(CAP):
        used = jnp.where(counts_ref[...] > c, dst_ref[c] + 1, 0)
        turn[pl.ds(16 * (n % 8) + c, 1), 0:N] = used.astype(F32)
    turned = turn[...].T
    for d in range(N):
        dmsg[d] = turned[d : d + 1].astype(jnp.int32)

    @pl.loop(0, 15)
    def _(step):
        d_send(to_node(step)).start()

    for k in range(1, LOOK):

        @pl.loop(0, 15)
        def _(step):
            z_send(k, to_node(step)).start()

    a_copy(n).wait()
    products(n, zrecv_a, zrecv_b, n)

    dtgt[n] = dmsg[n]
    r32[...] = jnp.zeros_like(r32)
    perm[0] = placing(0)
    perm[1] = placing(1)
    perm_copy = pltpu.make_async_copy(perm.at[:, pl.ds(MOST, 128)], out_perm, perm_sem)
    perm_copy.start()
    w_copy.wait()

    for which, target in ((0, wt0), (1, wt1)):

        @pl.loop(0, 8)
        def _(i):
            at = pl.ds(pl.multiple_of(i * 128, 128), 128)
            for j in range(8):
                block = wbuf[which, at, 128 * j : 128 * j + 128]
                target[128 * j : 128 * j + 128, at] = block.T

    d_all().wait_recv()
    low, high = dtgt[0], dtgt[8]
    for s in range(1, 8):
        low, high = low + dtgt[s], high + dtgt[8 + s]
    wanted = jnp.concatenate([low, high], axis=1)
    place = lax.broadcasted_iota(jnp.int32, (TILES, 256), 0) + 1
    onehot[...] = (place == wanted).astype(F32).astype(BF16)

    def aggregate(k):
        nr = ROWS[k]
        got = part(zrecv_a, zrecv_b, k)

        def unpack(s):
            if nr == 16:
                for c in range(CAP):
                    r32[pl.ds(s * 16 + c, 16, stride=256), :] = got[s, c].astype(F32)
            else:
                for c in range(0, CAP, 2):
                    both = got[s, c // 2].astype(F32)
                    r32[pl.ds(s * 16 + c, 8, stride=256), :] = both[:8]
                    r32[pl.ds(s * 16 + c + 1, 8, stride=256), :] = both[8:]

        unpack(n)

        @pl.loop(0, 15)
        def _(step):
            s = from_node(step)
            z_recv(k, s).wait_recv()
            if k + LOOK < len(ROWS):
                z_send(k + LOOK, to_node(step)).start()
            unpack(s)

        def rows_of(r):
            return r32[pl.ds(pl.multiple_of(r * 256, 256), 256), :]

        @pl.loop(0, nr // 4)
        def _(quarter):
            for pair in range(2):
                r = quarter * 4 + 2 * pair
                x = jnp.concatenate([rows_of(r), rows_of(r + 1)], axis=1).astype(BF16)
                sums = jnp.dot(onehot[...], x, preferred_element_type=F32)
                g32[pl.ds(r, TILES, stride=nr), :] = sums[:, :128]
                g32[pl.ds(r + 1, TILES, stride=nr), :] = sums[:, 128:]

        def packed(i):
            return g32[pl.ds(pl.multiple_of(i * 8 * nr, 8 * nr), 8 * nr), :].astype(BF16)

        out, mine = part(asend_a, asend_b, k), part(arecv_a, arecv_b, k)
        for to in across:
            out[to] = packed(to)
            g_send(k, to).start()
        mine[f] = packed(f)

    def self_part():
        own_self.wait()
        s_all().wait_recv()

        @pl.loop(0, 4)
        def _(i):
            at = pl.ds(pl.multiple_of(i * 256, 256), 256)
            by8 = [0.0] * B
            for tq in range(2):
                x = srecv[pl.ds(i * 4, 4), :, 512 * tq : 512 * tq + 512].reshape(256, 512)
                moved = lax.dot_general(x, perm[tq], NT, preferred_element_type=F32)
                for k in range(A):
                    selfp_a[k, at, 128 * tq : 128 * tq + 128] = moved[:, 128 * k : 128 * k + 128].astype(BF16)
                for k in range(B):
                    by8[k] = by8[k] + moved[:, 128 * (A + k) : 128 * (A + k) + 128]
            for k in range(B):
                selfp_b[k, at, :] = by8[k].astype(BF16)

        for k in range(A):
            hs_a[k] = jnp.dot(wt1[...], selfp_a[k], preferred_element_type=F32)
        for k in range(B):
            hs_b[k] = jnp.dot(wt1[...], selfp_b[k], preferred_element_type=F32)

    def layer(k):
        nr = ROWS[k]
        wide = 16 * nr
        g_all(k).wait_recv()
        got = part(arecv_a, arecv_b, k)
        lane = lax.broadcasted_iota(jnp.int32, (8 * nr, 128), 1)
        for m in range(8):
            a, b = got[2 * m].astype(F32), got[2 * m + 1].astype(F32)
            first = jnp.where(lane < 64, a, pltpu.roll(b, 64, 1)).astype(BF16)
            second = jnp.where(lane < 64, pltpu.roll(a, 64, 1), b).astype(BF16)
            cols = slice(128 * m, 128 * m + 128)
            for tq in range(2):
                at, of = 8 * nr * tq, slice(4 * nr * tq, 4 * nr * tq + 4 * nr)
                lhs[at : at + 4 * nr, cols] = first[of]
                lhs[at + 4 * nr : at + 8 * nr, cols] = second[of]

        here, away = part(hs_a, hs_b, k), part(bsend_a, bsend_b, k)
        total = jnp.zeros((1, wide), F32)
        for at in range(0, D, D // 2):
            half = slice(at, at + D // 2)
            hidden = here[half] + lax.dot_general(wt0[half], lhs[0:wide], NT, preferred_element_type=F32)
            active = jnp.maximum(hidden, 0.0)
            act[half, 0:wide] = active
            total = total + jnp.sum(active * active, axis=0, keepdims=True)
        scale = lax.rsqrt(total / D + 1e-06)
        for to in across:
            away[rows(to)] = (act[rows(to), 0:wide] * scale).astype(BF16)
            b_send(k, to).start()
        away[rows(f)] = (act[rows(f), 0:wide] * scale).astype(BF16)
        b_own(k).start()

    for step, k in SCHEDULE:
        if step == "sum":
            aggregate(k)
        else:
            if k == 0:
                self_part()
            layer(k)

    for k in range(LAST):
        b_own(k).wait()
        b_all(k).wait_recv()

    def most_copy(i):
        at = pl.ds(pl.multiple_of(i * 4 * SHARE, 4 * SHARE), 4 * SHARE)
        return pltpu.make_async_copy(most.at[:, at], out_most.at[:, at], most_sem.at[i])

    @pl.loop(0, 4)
    def _(i):
        of = pl.ds(pl.multiple_of(i * 256, 256), 256)
        for tq in range(2):
            x = [brecv_a[k, of, 128 * tq : 128 * tq + 128] for k in range(A)] + [brecv_b[k, of, :] for k in range(B - 1)]
            moved = jnp.dot(jnp.concatenate(x, axis=1), perm[tq, 0:MOST], preferred_element_type=F32).astype(BF16)
            for j in range(4):
                at = pl.multiple_of((i * 4 + j) * SHARE + 512 * tq, 512)
                most[:, pl.ds(at, 512)] = moved[C * j : C * j + C]
        most_copy(i).start()

    perm_copy.wait()
    d_all().wait_send()
    s_all().wait_send()
    for k in range(len(ROWS)):
        z_all(k).wait_send()
        g_all(k).wait_send()
        b_all(k).wait_send()
    for i in range(4):
        most_copy(i).wait()
    b_own(LAST).wait()
    b_all(LAST).wait_recv()


def place_kernel(most_ref, last_ref, perm_ref, out_ref, mbuf, lbuf, pbuf, obuf, m_sem, l_sem, p_sem, o_sem):
    def block(i):
        return pl.ds(4 * SHARE * i, 4 * SHARE)

    def fetch(i):
        return pltpu.make_async_copy(most_ref.at[:, block(i)], mbuf.at[i], m_sem.at[i])

    def store(i):
        return pltpu.make_async_copy(obuf.at[i], out_ref.at[:, block(i)], o_sem.at[i])

    fetch_perm = pltpu.make_async_copy(perm_ref, pbuf, p_sem)
    fetch_last = pltpu.make_async_copy(last_ref, lbuf, l_sem)
    fetch_perm.start()
    fetch_last.start()
    for i in range(4):
        fetch(i).start()
    fetch_perm.wait()
    fetch_last.wait()
    for i in range(4):
        fetch(i).wait()
        for tq in range(2):
            moved = jnp.dot(lbuf[256 * i : 256 * i + 256], pbuf[tq], preferred_element_type=F32)
            for j in range(4):
                at = slice(SHARE * j + 512 * tq, SHARE * j + 512 * tq + 512)
                obuf[i, :, at] = (mbuf[i, :, at].astype(F32) + moved[C * j : C * j + C]).astype(BF16)
        store(i).start()
    for i in range(4):
        store(i).wait()


def on_device(features, tile_vals, src_tile, dst_tile, counts, weight):
    hbm = pl.BlockSpec(memory_space=pl.ANY)
    vmem = pl.BlockSpec(memory_space=pltpu.VMEM)
    smem = pl.BlockSpec(memory_space=pltpu.SMEM)
    dma = pltpu.SemaphoreType.DMA
    chunks = len(ROWS)

    def both(rows_a, rows_b, kind=BF16):
        return [pltpu.VMEM((A, *rows_a), kind), pltpu.VMEM((B, *rows_b), kind)]

    most, last, perm = pl.pallas_call(
        kernel,
        out_shape=(
            jax.ShapeDtypeStruct((C, TILES * T), BF16),
            jax.ShapeDtypeStruct((D, 128), BF16),
            jax.ShapeDtypeStruct((2, 128, 512), BF16),
        ),
        in_specs=[smem, vmem, vmem, hbm, hbm, hbm],
        out_specs=(hbm, hbm, hbm),
        scratch_shapes=[
            pltpu.VMEM((C, TILES * T), BF16),
            pltpu.VMEM((TILES, C, T), BF16),
            pltpu.VMEM((N, CAP, T, T), BF16),
            pltpu.VMEM((2, D, D), BF16),
            pltpu.VMEM((D, D), BF16),
            pltpu.VMEM((D, D), BF16),
            *both((N, CAP, 16, 128), (N, CAP // 2, 16, 128)),
            *both((N, CAP, 16, 128), (N, CAP // 2, 16, 128)),
            pltpu.VMEM((128, 128), F32),
            pltpu.VMEM((N, 1, 128), jnp.int32),
            pltpu.VMEM((N, 1, 128), jnp.int32),
            pltpu.VMEM((16 * 256, 128), F32),
            pltpu.VMEM((TILES * 16, 128), F32),
            *both((F, 128, 128), (F, 64, 128)),
            *both((F, 128, 128), (F, 64, 128)),
            pltpu.VMEM((F, C, SHARE), BF16),
            *both((D, 256), (D, 128)),
            *both((D, 256), (D, 128), F32),
            pltpu.VMEM((256, D), BF16),
            pltpu.VMEM((D, 256), F32),
            *both((D, 256), (D, 128)),
            pltpu.VMEM((A, D, 256), BF16),
            pltpu.VMEM((B - 1, D, 128), BF16),
            pltpu.VMEM((C, TILES * T), BF16),
            pltpu.VMEM((2, LANES, 512), BF16),
            pltpu.VMEM((TILES, 256), BF16),
            dma,
            dma((N,)),
            dma,
            dma,
            dma,
            dma((4,)),
            dma((chunks,)),
            dma,
            dma,
            dma,
            dma,
            dma((chunks,)),
            dma((chunks, N)),
            dma((chunks,)),
            dma((chunks,)),
            dma((chunks,)),
            dma((chunks,)),
        ],
        compiler_params=pltpu.CompilerParams(collective_id=1, has_side_effects=True, vmem_limit_bytes=60 * 2**20),
    )(src_tile.transpose(2, 0, 1), dst_tile.transpose(2, 0, 1), counts, features.T, tile_vals[0], weight)
    out = pl.pallas_call(
        place_kernel,
        out_shape=jax.ShapeDtypeStruct((C, TILES * T), BF16),
        in_specs=[hbm, hbm, hbm],
        out_specs=hbm,
        scratch_shapes=[
            pltpu.VMEM((4, C, 4 * SHARE), BF16),
            pltpu.VMEM((D, 128), BF16),
            pltpu.VMEM((2, 128, 512), BF16),
            pltpu.VMEM((4, C, 4 * SHARE), BF16),
            dma((4,)),
            dma,
            dma,
            dma((4,)),
        ],
        compiler_params=pltpu.CompilerParams(vmem_limit_bytes=60 * 2**20),
    )(most, last, perm)
    return out.T


def solution(mesh):
    return jax.shard_map(
        on_device,
        mesh=mesh,
        in_specs=(
            P("nodes", "feat"),
            P("nodes", None, None, None, None),
            P("nodes", None, None),
            P("nodes", None, None),
            P("nodes", None),
            P(),
        ),
        out_specs=P("nodes", "feat"),
        check_vma=False,
    )
```

```python
import jax
import jax.numpy as jnp
from jax import lax
from jax.experimental import pallas as pl
from jax.experimental.pallas import tpu as pltpu
from jax.sharding import PartitionSpec as P

MESH = pl.DeviceIdType.MESH
BF16, F32 = jnp.bfloat16, jnp.float32
N = 16
F = 16
CAP = 12
T = 128
TILES = 128
C = 64
D = 1024
SHARE = 1024
ROWS = (16, 16, 16, 8, 8)
A, B = 3, 2
LOOK = 2
LAST = len(ROWS) - 1
LANES = 128 * (A + B)
MOST = 128 * LAST
CHUNKS = [(0, a) for a in range(A)] + [(1, b) for b in range(B)]

NT = (((1,), (1,)), ((), ()))

def node_partner(n, step, sign):
    j = lax.div(step, 2)
    dz = 4 + (2 * lax.rem(j, 2) - 1) * lax.div(j + 1, 2)
    return lax.rem(lax.div(n, 2) + 8 + sign * dz, 8) * 2 + lax.rem(n + step + 1, 2)


def feat_partner(f, offset):
    dy, dx = offset
    return lax.rem(lax.div(f, 4) + dy, 4) * 4 + lax.rem(lax.rem(f, 4) + dx, 4)


def placing(tq):
    lane = lax.broadcasted_iota(jnp.int32, (LANES, 512), 0)
    row = lax.broadcasted_iota(jnp.int32, (LANES, 512), 1)
    tl, h, i = row // 128, (row // 64) % 2, row % 64
    by16 = (i // 16) * 128 + h * 64 + tl * 16 + i % 16
    by8 = A * 128 + ((i - 16 * A) // 8) * 128 + tq * 64 + h * 32 + tl * 8 + i % 8
    return (lane == jnp.where(i < 16 * A, by16, by8)).astype(F32).astype(BF16)


def kernel(
    src_ref,
    dst_ref,
    counts_ref,
    xt_ref,
    a_ref,
    w_ref,
    out_most,
    out_last,
    out_perm,
    xbuf,
    xtile,
    abuf,
    wbuf,
    wt0,
    wt1,
    zsend_a,
    zsend_b,
    zrecv_a,
    zrecv_b,
    turn,
    dmsg,
    dtgt,
    r32,
    g32,
    asend_a,
    asend_b,
    arecv_a,
    arecv_b,
    srecv,
    selfp_a,
    selfp_b,
    hs_a,
    hs_b,
    lhs,
    act,
    bsend_a,
    bsend_b,
    brecv_a,
    brecv_b,
    most,
    perm,
    onehot,
    xsem,
    asem,
    wsem,
    own_sem,
    perm_sem,
    most_sem,
    back_sem,
    d_ss,
    d_rs,
    s_ss,
    s_rs,
    z_ss,
    z_rs,
    g_ss,
    g_rs,
    b_ss,
    b_rs,
):
    n, f = lax.axis_index("nodes"), lax.axis_index("feat")

    def node(i):
        return (i, f)

    def col(i):
        return (n, i)

    def to_node(step):
        return node_partner(n, step, 1)

    def from_node(step):
        return node_partner(n, step, -1)

    def part(a, b, k):
        return (b if k[0] else a).at[k[1]]

    def num(k):
        return A * k[0] + k[1]

    def across(step):
        s = step + lax.div(step, 10)
        return feat_partner(f, (2 + lax.div(s, 4), 2 + lax.rem(s, 4)))

    def back(k):
        return out_last if k == "last" else part(brecv_a, brecv_b, k)

    x_copy = pltpu.make_async_copy(xt_ref, xbuf, xsem)
    x_copy.start()

    def a_copy(d):
        return pltpu.make_async_copy(a_ref.at[d], abuf.at[d], asem.at[d])

    @pl.loop(0, 16)
    def _(step):
        a_copy(to_node(step)).start()

    w_copy = pltpu.make_async_copy(w_ref, wbuf, wsem)
    w_copy.start()

    barrier = pltpu.get_barrier_semaphore()

    @pl.loop(0, 15)
    def _(step):
        pl.semaphore_signal(barrier, inc=1, device_id=node(to_node(step)), device_id_type=MESH)

    @pl.loop(0, 15)
    def _(step):
        pl.semaphore_signal(barrier, inc=1, device_id=col(across(step)), device_id_type=MESH)

    x_copy.wait()

    @pl.loop(0, TILES, unroll=8)
    def _(t):
        xtile[t] = xbuf[:, pl.ds(pl.multiple_of(t * T, T), T)]

    def remote(src, dst, ss, rs, device):
        return pltpu.make_async_remote_copy(src, dst, ss, rs, device_id=device, device_id_type=MESH)

    def all_of(ref, size=1):
        return ref.at[pl.ds(0, 15 * size)]

    def d_send(to):
        return remote(dmsg.at[to], dtgt.at[n], d_ss, d_rs, node(to))

    def d_all():
        return remote(all_of(dmsg), all_of(dtgt), d_ss, d_rs, node(n))

    def share(i):
        return pl.ds(pl.multiple_of(i * SHARE, SHARE), SHARE)

    def s_send(to):
        return remote(xt_ref.at[:, share(to)], srecv.at[f], s_ss, s_rs, col(to))

    def s_all():
        return remote(all_of(srecv), all_of(srecv), s_ss, s_rs, col(f))

    def z_send(k, to):
        src, dst = part(zsend_a, zsend_b, k), part(zrecv_a, zrecv_b, k)
        return remote(src.at[to], dst.at[n], z_ss.at[num(k)], z_rs.at[num(k), n], node(to))

    def z_recv(k, frm):
        src, dst = part(zsend_a, zsend_b, k), part(zrecv_a, zrecv_b, k)
        return remote(src.at[frm], dst.at[frm], z_ss.at[num(k)], z_rs.at[num(k), frm], node(frm))

    def z_all(k):
        src, dst = part(zsend_a, zsend_b, k), part(zrecv_a, zrecv_b, k)
        return remote(all_of(src), all_of(dst), z_ss.at[num(k)], z_rs.at[num(k), n], node(n))

    def g_send(k, to):
        src, dst = part(asend_a, asend_b, k), part(arecv_a, arecv_b, k)
        return remote(src.at[to], dst.at[f], g_ss.at[num(k)], g_rs.at[num(k)], col(to))

    def g_all(k):
        src, dst = part(asend_a, asend_b, k), part(arecv_a, arecv_b, k)
        return remote(all_of(src), all_of(dst), g_ss.at[num(k)], g_rs.at[num(k)], col(f))

    def rows(i):
        return pl.ds(pl.multiple_of(i * C, C), C)

    def b_ends(k):
        last = k == "last"
        chunk = (1, B - 1) if last else k
        return part(bsend_a, bsend_b, chunk), back(k), num(chunk)

    def b_send(k, to):
        src, dst, c = b_ends(k)
        return remote(src.at[rows(to)], dst.at[rows(f)], b_ss.at[c], b_rs.at[c], col(to))

    def b_all(k):
        src, dst, c = b_ends(k)
        return remote(all_of(src, C), all_of(dst, C), b_ss.at[c], b_rs.at[c], col(f))

    def b_own(k):
        src, dst, c = b_ends(k)
        return pltpu.make_async_copy(src.at[rows(f)], dst.at[rows(f)], back_sem.at[c])

    none = jnp.zeros((C, T), BF16)

    def products(d, to_a, to_b, at):
        kept = None
        for c in range(CAP):
            a = abuf[d, c]
            left = jnp.concatenate([a[: T // 2], a[T // 2 :]], axis=1)
            x = xtile[src_ref[c, 0, d]]
            right = jnp.concatenate(
                [jnp.concatenate([x, none], axis=1), jnp.concatenate([none, x], axis=1)], axis=0
            )
            value = lax.dot_general(left, right, NT, preferred_element_type=F32)
            for k in range(A):
                to_a[k, at, c] = value[16 * k : 16 * k + 16].astype(BF16)
            if c % 2 == 0:
                kept = value
                continue
            for k in range(B):
                rows8 = slice(16 * A + 8 * k, 16 * A + 8 * k + 8)
                to_b[k, at, c // 2] = jnp.concatenate([kept[rows8], value[rows8]], axis=0).astype(BF16)

    def stage_one(step):
        d = to_node(step)
        a_copy(d).wait()
        products(d, zsend_a, zsend_b, d)

    stage_one(0)
    pl.semaphore_wait(barrier, 30)
    z_send((0, 0), to_node(0)).start()

    @pl.loop(0, 15)
    def _(step):
        s_send(across(step)).start()

    own_self = pltpu.make_async_copy(xt_ref.at[:, share(f)], srecv.at[f], own_sem)
    own_self.start()

    @pl.loop(1, 15)
    def _(step):
        stage_one(step)
        z_send((0, 0), to_node(step)).start()

    turn[...] = jnp.zeros_like(turn)
    for c in range(CAP):
        used = jnp.where(counts_ref[...] > c, dst_ref[c] + 1, 0)
        turn[pl.ds(16 * (n % 8) + c, 1), 0:N] = used.astype(F32)
    turned = turn[...].T
    for d in range(N):
        dmsg[d] = turned[d : d + 1].astype(jnp.int32)

    @pl.loop(0, 15)
    def _(step):
        d_send(to_node(step)).start()

    for k in range(1, LOOK):

        @pl.loop(0, 15)
        def _(step):
            z_send((0, k), to_node(step)).start()

    a_copy(n).wait()
    products(n, zrecv_a, zrecv_b, n)

    dtgt[n] = dmsg[n]
    r32[...] = jnp.zeros_like(r32)
    perm[0] = placing(0)
    perm[1] = placing(1)
    perm_copy = pltpu.make_async_copy(perm.at[:, pl.ds(MOST, 128)], out_perm, perm_sem)
    perm_copy.start()
    w_copy.wait()

    for which, target in ((0, wt0), (1, wt1)):

        @pl.loop(0, 8)
        def _(i):
            at = pl.ds(pl.multiple_of(i * 128, 128), 128)
            for j in range(8):
                block = wbuf[which, at, 128 * j : 128 * j + 128]
                target[128 * j : 128 * j + 128, at] = block.T

    d_all().wait_recv()
    low, high = dtgt[0], dtgt[8]
    for s in range(1, 8):
        low, high = low + dtgt[s], high + dtgt[8 + s]
    wanted = jnp.concatenate([low, high], axis=1)
    place = lax.broadcasted_iota(jnp.int32, (TILES, 256), 0) + 1
    onehot[...] = (place == wanted).astype(F32).astype(BF16)

    def aggregate(k):
        nr = (16, 8)[k[0]]
        got = part(zrecv_a, zrecv_b, k)

        def unpack(s):
            if nr == 16:
                for c in range(CAP):
                    r32[pl.ds(s * 16 + c, 16, stride=256), :] = got[s, c].astype(F32)
            else:
                for c in range(0, CAP, 2):
                    both = got[s, c // 2].astype(F32)
                    r32[pl.ds(s * 16 + c, 8, stride=256), :] = both[:8]
                    r32[pl.ds(s * 16 + c + 1, 8, stride=256), :] = both[8:]

        unpack(n)

        @pl.loop(0, 15)
        def _(step):
            s = from_node(step)
            z_recv(k, s).wait_recv()
            if k[0] == 0:

                @pl.when(k[1] + LOOK < A)
                def _():
                    z_send((0, k[1] + LOOK), to_node(step)).start()

                @pl.when(k[1] + LOOK >= A)
                def _():
                    z_send((1, k[1] + LOOK - A), to_node(step)).start()

            unpack(s)

        def rows_of(r):
            return r32[pl.ds(pl.multiple_of(r * 256, 256), 256), :]

        @pl.loop(0, nr // 4)
        def _(quarter):
            for pair in range(2):
                r = quarter * 4 + 2 * pair
                x = jnp.concatenate([rows_of(r), rows_of(r + 1)], axis=1).astype(BF16)
                sums = jnp.dot(onehot[...], x, preferred_element_type=F32)
                g32[pl.ds(r, TILES, stride=nr), :] = sums[:, :128]
                g32[pl.ds(r + 1, TILES, stride=nr), :] = sums[:, 128:]

        def packed(i):
            return g32[pl.ds(pl.multiple_of(i * 8 * nr, 8 * nr), 8 * nr), :].astype(BF16)

        out, mine = part(asend_a, asend_b, k), part(arecv_a, arecv_b, k)

        @pl.loop(0, 15)
        def _(step):
            to = across(step)
            out[to] = packed(to)
            g_send(k, to).start()

        mine[f] = packed(f)

    def self_part():
        own_self.wait()
        s_all().wait_recv()

        @pl.loop(0, 4)
        def _(i):
            at = pl.ds(pl.multiple_of(i * 256, 256), 256)
            by8 = [0.0] * B
            for tq in range(2):
                x = srecv[pl.ds(i * 4, 4), :, 512 * tq : 512 * tq + 512].reshape(256, 512)
                moved = lax.dot_general(x, perm[tq], NT, preferred_element_type=F32)
                for k in range(A):
                    selfp_a[k, at, 128 * tq : 128 * tq + 128] = moved[:, 128 * k : 128 * k + 128].astype(BF16)
                for k in range(B):
                    by8[k] = by8[k] + moved[:, 128 * (A + k) : 128 * (A + k) + 128]
            for k in range(B):
                selfp_b[k, at, :] = by8[k].astype(BF16)

        for k in range(A):
            hs_a[k] = jnp.dot(wt1[...], selfp_a[k], preferred_element_type=F32)
        for k in range(B):
            hs_b[k] = jnp.dot(wt1[...], selfp_b[k], preferred_element_type=F32)

    def layer(k):
        nr = (16, 8)[k[0]]
        wide = 16 * nr
        g_all(k).wait_recv()
        got = part(arecv_a, arecv_b, k)
        lane = lax.broadcasted_iota(jnp.int32, (8 * nr, 128), 1)
        for m in range(8):
            a, b = got[2 * m].astype(F32), got[2 * m + 1].astype(F32)
            first = jnp.where(lane < 64, a, pltpu.roll(b, 64, 1)).astype(BF16)
            second = jnp.where(lane < 64, pltpu.roll(a, 64, 1), b).astype(BF16)
            cols = slice(128 * m, 128 * m + 128)
            for tq in range(2):
                at, of = 8 * nr * tq, slice(4 * nr * tq, 4 * nr * tq + 4 * nr)
                lhs[at : at + 4 * nr, cols] = first[of]
                lhs[at + 4 * nr : at + 8 * nr, cols] = second[of]

        here, away = part(hs_a, hs_b, k), part(bsend_a, bsend_b, k)
        total = jnp.zeros((1, wide), F32)
        for at in range(0, D, D // 2):
            half = slice(at, at + D // 2)
            hidden = here[half] + lax.dot_general(wt0[half], lhs[0:wide], NT, preferred_element_type=F32)
            active = jnp.maximum(hidden, 0.0)
            act[half, 0:wide] = active
            total = total + jnp.sum(active * active, axis=0, keepdims=True)
        scale = lax.rsqrt(total / D + 1e-06)

        def send_back(k):
            @pl.loop(0, 15)
            def _(step):
                to = across(step)
                away[rows(to)] = (act[rows(to), 0:wide] * scale).astype(BF16)
                b_send(k, to).start()

            away[rows(f)] = (act[rows(f), 0:wide] * scale).astype(BF16)
            b_own(k).start()

        if k[0] == 0:
            send_back(k)
        else:

            @pl.when(k[1] < B - 1)
            def _():
                send_back((1, 0))

            @pl.when(k[1] == B - 1)
            def _():
                send_back("last")

    @pl.loop(0, 10)
    def _(step):
        @pl.when((step == 0) | (step == 2) | (step == 4))
        def _():
            aggregate((0, lax.div(step, 2)))

        @pl.when(step == 0)
        def _():
            self_part()

        @pl.when((step == 1) | (step == 3) | (step == 6))
        def _():
            layer((0, lax.div(step, 3)))

        @pl.when((step == 5) | (step == 8))
        def _():
            aggregate((1, lax.div(step - 5, 3)))

        @pl.when((step == 7) | (step == 9))
        def _():
            layer((1, lax.div(step - 7, 2)))

    for k in CHUNKS[:LAST]:
        b_own(k).wait()
        b_all(k).wait_recv()

    def most_copy(i):
        at = pl.ds(pl.multiple_of(i * 4 * SHARE, 4 * SHARE), 4 * SHARE)
        return pltpu.make_async_copy(most.at[:, at], out_most.at[:, at], most_sem.at[i])

    @pl.loop(0, 4)
    def _(i):
        of = pl.ds(pl.multiple_of(i * 256, 256), 256)
        for tq in range(2):
            x = [brecv_a[k, of, 128 * tq : 128 * tq + 128] for k in range(A)] + [brecv_b[k, of, :] for k in range(B - 1)]
            moved = jnp.dot(jnp.concatenate(x, axis=1), perm[tq, 0:MOST], preferred_element_type=F32).astype(BF16)
            for j in range(4):
                at = pl.multiple_of((i * 4 + j) * SHARE + 512 * tq, 512)
                most[:, pl.ds(at, 512)] = moved[C * j : C * j + C]
        most_copy(i).start()

    perm_copy.wait()
    d_all().wait_send()
    s_all().wait_send()
    for k in CHUNKS:
        z_all(k).wait_send()
        g_all(k).wait_send()
        b_all("last" if k == CHUNKS[LAST] else k).wait_send()
    for i in range(4):
        most_copy(i).wait()
    b_own("last").wait()
    b_all("last").wait_recv()


def place_kernel(most_ref, last_ref, perm_ref, out_ref, mbuf, lbuf, pbuf, obuf, m_sem, l_sem, p_sem, o_sem):
    def block(i):
        return pl.ds(4 * SHARE * i, 4 * SHARE)

    def fetch(i):
        return pltpu.make_async_copy(most_ref.at[:, block(i)], mbuf.at[i], m_sem.at[i])

    def store(i):
        return pltpu.make_async_copy(obuf.at[i], out_ref.at[:, block(i)], o_sem.at[i])

    fetch_perm = pltpu.make_async_copy(perm_ref, pbuf, p_sem)
    fetch_last = pltpu.make_async_copy(last_ref, lbuf, l_sem)
    fetch_perm.start()
    fetch_last.start()
    for i in range(4):
        fetch(i).start()
    fetch_perm.wait()
    fetch_last.wait()
    for i in range(4):
        fetch(i).wait()
        for tq in range(2):
            moved = jnp.dot(lbuf[256 * i : 256 * i + 256], pbuf[tq], preferred_element_type=F32)
            for j in range(4):
                at = slice(SHARE * j + 512 * tq, SHARE * j + 512 * tq + 512)
                obuf[i, :, at] = (mbuf[i, :, at].astype(F32) + moved[C * j : C * j + C]).astype(BF16)
        store(i).start()
    for i in range(4):
        store(i).wait()


def on_device(features, tile_vals, src_tile, dst_tile, counts, weight):
    hbm = pl.BlockSpec(memory_space=pl.ANY)
    vmem = pl.BlockSpec(memory_space=pltpu.VMEM)
    smem = pl.BlockSpec(memory_space=pltpu.SMEM)
    dma = pltpu.SemaphoreType.DMA
    chunks = len(ROWS)

    def both(rows_a, rows_b, kind=BF16):
        return [pltpu.VMEM((A, *rows_a), kind), pltpu.VMEM((B, *rows_b), kind)]

    most, last, perm = pl.pallas_call(
        kernel,
        out_shape=(
            jax.ShapeDtypeStruct((C, TILES * T), BF16),
            jax.ShapeDtypeStruct((D, 128), BF16),
            jax.ShapeDtypeStruct((2, 128, 512), BF16),
        ),
        in_specs=[smem, vmem, vmem, hbm, hbm, hbm],
        out_specs=(hbm, hbm, hbm),
        scratch_shapes=[
            pltpu.VMEM((C, TILES * T), BF16),
            pltpu.VMEM((TILES, C, T), BF16),
            pltpu.VMEM((N, CAP, T, T), BF16),
            pltpu.VMEM((2, D, D), BF16),
            pltpu.VMEM((D, D), BF16),
            pltpu.VMEM((D, D), BF16),
            *both((N, CAP, 16, 128), (N, CAP // 2, 16, 128)),
            *both((N, CAP, 16, 128), (N, CAP // 2, 16, 128)),
            pltpu.VMEM((128, 128), F32),
            pltpu.VMEM((N, 1, 128), jnp.int32),
            pltpu.VMEM((N, 1, 128), jnp.int32),
            pltpu.VMEM((16 * 256, 128), F32),
            pltpu.VMEM((TILES * 16, 128), F32),
            *both((F, 128, 128), (F, 64, 128)),
            *both((F, 128, 128), (F, 64, 128)),
            pltpu.VMEM((F, C, SHARE), BF16),
            *both((D, 256), (D, 128)),
            *both((D, 256), (D, 128), F32),
            pltpu.VMEM((256, D), BF16),
            pltpu.VMEM((D, 256), F32),
            *both((D, 256), (D, 128)),
            pltpu.VMEM((A, D, 256), BF16),
            pltpu.VMEM((B - 1, D, 128), BF16),
            pltpu.VMEM((C, TILES * T), BF16),
            pltpu.VMEM((2, LANES, 512), BF16),
            pltpu.VMEM((TILES, 256), BF16),
            dma,
            dma((N,)),
            dma,
            dma,
            dma,
            dma((4,)),
            dma((chunks,)),
            dma,
            dma,
            dma,
            dma,
            dma((chunks,)),
            dma((chunks, N)),
            dma((chunks,)),
            dma((chunks,)),
            dma((chunks,)),
            dma((chunks,)),
        ],
        compiler_params=pltpu.CompilerParams(collective_id=1, has_side_effects=True, vmem_limit_bytes=60 * 2**20),
    )(src_tile.transpose(2, 0, 1), dst_tile.transpose(2, 0, 1), counts, features.T, tile_vals[0], weight)
    out = pl.pallas_call(
        place_kernel,
        out_shape=jax.ShapeDtypeStruct((C, TILES * T), BF16),
        in_specs=[hbm, hbm, hbm],
        out_specs=hbm,
        scratch_shapes=[
            pltpu.VMEM((4, C, 4 * SHARE), BF16),
            pltpu.VMEM((D, 128), BF16),
            pltpu.VMEM((2, 128, 512), BF16),
            pltpu.VMEM((4, C, 4 * SHARE), BF16),
            dma((4,)),
            dma,
            dma,
            dma((4,)),
        ],
        compiler_params=pltpu.CompilerParams(vmem_limit_bytes=60 * 2**20),
    )(most, last, perm)
    return out.T


def solution(mesh):
    return jax.shard_map(
        on_device,
        mesh=mesh,
        in_specs=(
            P("nodes", "feat"),
            P("nodes", None, None, None, None),
            P("nodes", None, None),
            P("nodes", None, None),
            P("nodes", None),
            P(),
        ),
        out_specs=P("nodes", "feat"),
        check_vma=False,
    )
```

```python
import jax
import jax.numpy as jnp
from jax import lax
from jax.experimental import pallas as pl
from jax.experimental.pallas import tpu as pltpu
from jax.sharding import PartitionSpec as P

MESH = pl.DeviceIdType.MESH
BF16, F32 = jnp.bfloat16, jnp.float32
N = 16
F = 16
CAP = 12
T = 128
TILES = 128
C = 64
D = 1024
SHARE = 1024
ROWS = (16, 16, 16, 8, 8)
A, B = 3, 2
LOOK = 2
LAST = len(ROWS) - 1
LANES = 128 * (A + B)
MOST = 128 * LAST
SCHEDULE = (
    ("sum", 0), ("layer", 0), ("sum", 1), ("layer", 1), ("sum", 2), ("sum", 3), ("layer", 2), ("layer", 3), ("sum", 4), ("layer", 4),
)

NT = (((1,), (1,)), ((), ()))

FAR = sorted(
    [(dy, dx) for dy in range(4) for dx in range(4) if (dy, dx) != (0, 0)],
    key=lambda o: -(min(o[0], 4 - o[0]) + min(o[1], 4 - o[1])),
)


def node_partner(n, step, sign):
    if isinstance(step, int):
        j = step // 2
        dz = 4 + (2 * (j % 2) - 1) * ((j + 1) // 2)
    else:
        j = lax.div(step, 2)
        dz = 4 + (2 * lax.rem(j, 2) - 1) * lax.div(j + 1, 2)
    return lax.rem(lax.div(n, 2) + (8 + sign * dz), 8) * 2 + lax.rem(n + (step + 1), 2)


def feat_partner(f, offset):
    dy, dx = offset
    return lax.rem(lax.div(f, 4) + dy, 4) * 4 + lax.rem(lax.rem(f, 4) + dx, 4)


def placing(tq):
    lane = lax.broadcasted_iota(jnp.int32, (LANES, 512), 0)
    row = lax.broadcasted_iota(jnp.int32, (LANES, 512), 1)
    tl, h, i = row // 128, (row // 64) % 2, row % 64
    by16 = (i // 16) * 128 + h * 64 + tl * 16 + i % 16
    by8 = A * 128 + ((i - 16 * A) // 8) * 128 + tq * 64 + h * 32 + tl * 8 + i % 8
    return (lane == jnp.where(i < 16 * A, by16, by8)).astype(F32).astype(BF16)


def kernel(
    src_ref,
    dst_ref,
    counts_ref,
    xt_ref,
    a_ref,
    w_ref,
    out_most,
    out_last,
    out_perm,
    xbuf,
    xtile,
    abuf,
    wbuf,
    wt0,
    wt1,
    zsend_a,
    zsend_b,
    zrecv_a,
    zrecv_b,
    turn,
    dmsg,
    dtgt,
    r32,
    g32,
    asend_a,
    asend_b,
    arecv_a,
    arecv_b,
    srecv,
    selfp_a,
    selfp_b,
    hs_a,
    hs_b,
    lhs,
    act,
    bsend_a,
    bsend_b,
    brecv_a,
    brecv_b,
    most,
    perm,
    onehot,
    xsem,
    asem,
    wsem,
    own_sem,
    perm_sem,
    most_sem,
    back_sem,
    d_ss,
    d_rs,
    s_ss,
    s_rs,
    z_ss,
    z_rs,
    g_ss,
    g_rs,
    b_ss,
    b_rs,
):
    n, f = lax.axis_index("nodes"), lax.axis_index("feat")
    across = [feat_partner(f, o) for o in FAR]

    def node(i):
        return (i, f)

    def col(i):
        return (n, i)

    def to_node(step):
        return node_partner(n, step, 1)

    receivers = [to_node(step) for step in range(15)]
    senders = [node_partner(n, step, -1) for step in range(15)]

    def part(a, b, k):
        return a.at[k] if k < A else b.at[k - A]

    def back(k):
        return out_last if k == LAST else part(brecv_a, brecv_b, k)

    x_copy = pltpu.make_async_copy(xt_ref, xbuf, xsem)
    x_copy.start()

    def a_copy(d):
        return pltpu.make_async_copy(a_ref.at[d], abuf.at[d], asem.at[d])

    @pl.loop(0, 16)
    def _(step):
        a_copy(to_node(step)).start()

    w_copy = pltpu.make_async_copy(w_ref, wbuf, wsem)
    w_copy.start()

    barrier = pltpu.get_barrier_semaphore()

    for to in receivers:
        pl.semaphore_signal(barrier, inc=1, device_id=node(to), device_id_type=MESH)

    for to in across:
        pl.semaphore_signal(barrier, inc=1, device_id=col(to), device_id_type=MESH)

    x_copy.wait()

    @pl.loop(0, TILES, unroll=8)
    def _(t):
        xtile[t] = xbuf[:, pl.ds(pl.multiple_of(t * T, T), T)]

    def remote(src, dst, ss, rs, device):
        return pltpu.make_async_remote_copy(src, dst, ss, rs, device_id=device, device_id_type=MESH)

    def all_of(ref, size=1):
        return ref.at[pl.ds(0, 15 * size)]

    def d_send(to):
        return remote(dmsg.at[to], dtgt.at[n], d_ss, d_rs, node(to))

    def d_all():
        return remote(all_of(dmsg), all_of(dtgt), d_ss, d_rs, node(n))

    def share(i):
        return pl.ds(pl.multiple_of(i * SHARE, SHARE), SHARE)

    def s_send(to):
        return remote(xt_ref.at[:, share(to)], srecv.at[f], s_ss, s_rs, col(to))

    def s_all():
        return remote(all_of(srecv), all_of(srecv), s_ss, s_rs, col(f))

    def z_send(k, to):
        src, dst = part(zsend_a, zsend_b, k), part(zrecv_a, zrecv_b, k)
        return remote(src.at[to], dst.at[n], z_ss.at[k], z_rs.at[k, n], node(to))

    def z_recv(k, frm):
        src, dst = part(zsend_a, zsend_b, k), part(zrecv_a, zrecv_b, k)
        return remote(src.at[frm], dst.at[frm], z_ss.at[k], z_rs.at[k, frm], node(frm))

    def z_all(k):
        src, dst = part(zsend_a, zsend_b, k), part(zrecv_a, zrecv_b, k)
        return remote(all_of(src), all_of(dst), z_ss.at[k], z_rs.at[k, n], node(n))

    def g_send(k, to):
        src, dst = part(asend_a, asend_b, k), part(arecv_a, arecv_b, k)
        return remote(src.at[to], dst.at[f], g_ss.at[k], g_rs.at[k], col(to))

    def g_all(k):
        src, dst = part(asend_a, asend_b, k), part(arecv_a, arecv_b, k)
        return remote(all_of(src), all_of(dst), g_ss.at[k], g_rs.at[k], col(f))

    def rows(i):
        return pl.ds(pl.multiple_of(i * C, C), C)

    def b_send(k, to):
        src, dst = part(bsend_a, bsend_b, k), back(k)
        return remote(src.at[rows(to)], dst.at[rows(f)], b_ss.at[k], b_rs.at[k], col(to))

    def b_all(k):
        src, dst = part(bsend_a, bsend_b, k), back(k)
        return remote(all_of(src, C), all_of(dst, C), b_ss.at[k], b_rs.at[k], col(f))

    def b_own(k):
        src, dst = part(bsend_a, bsend_b, k), back(k)
        return pltpu.make_async_copy(src.at[rows(f)], dst.at[rows(f)], back_sem.at[k])

    none = jnp.zeros((C, T), BF16)

    def products(d, to_a, to_b, at):
        kept = None
        for c in range(CAP):
            a = abuf[d, c]
            left = jnp.concatenate([a[: T // 2], a[T // 2 :]], axis=1)
            x = xtile[src_ref[c, 0, d]]
            right = jnp.concatenate(
                [jnp.concatenate([x, none], axis=1), jnp.concatenate([none, x], axis=1)], axis=0
            )
            value = lax.dot_general(left, right, NT, preferred_element_type=F32)
            for k in range(A):
                to_a[k, at, c] = value[16 * k : 16 * k + 16].astype(BF16)
            if c % 2 == 0:
                kept = value
                continue
            for k in range(B):
                rows8 = slice(16 * A + 8 * k, 16 * A + 8 * k + 8)
                to_b[k, at, c // 2] = jnp.concatenate([kept[rows8], value[rows8]], axis=0).astype(BF16)

    def stage_one(step):
        d = to_node(step)
        a_copy(d).wait()
        products(d, zsend_a, zsend_b, d)

    stage_one(0)
    pl.semaphore_wait(barrier, 30)
    z_send(0, to_node(0)).start()

    for to in across:
        s_send(to).start()

    own_self = pltpu.make_async_copy(xt_ref.at[:, share(f)], srecv.at[f], own_sem)
    own_self.start()

    @pl.loop(1, 15)
    def _(step):
        stage_one(step)
        z_send(0, to_node(step)).start()

    turn[...] = jnp.zeros_like(turn)
    for c in range(CAP):
        used = jnp.where(counts_ref[...] > c, dst_ref[c] + 1, 0)
        turn[pl.ds(16 * (n % 8) + c, 1), 0:N] = used.astype(F32)
    turned = turn[...].T
    for d in range(N):
        dmsg[d] = turned[d : d + 1].astype(jnp.int32)

    for to in receivers:
        d_send(to).start()

    for k in range(1, LOOK):
        for to in receivers:
            z_send(k, to).start()

    a_copy(n).wait()
    products(n, zrecv_a, zrecv_b, n)

    dtgt[n] = dmsg[n]
    r32[...] = jnp.zeros_like(r32)
    perm[0] = placing(0)
    perm[1] = placing(1)
    perm_copy = pltpu.make_async_copy(perm.at[:, pl.ds(MOST, 128)], out_perm, perm_sem)
    perm_copy.start()
    w_copy.wait()

    for which, target in ((0, wt0), (1, wt1)):

        @pl.loop(0, 8)
        def _(i):
            at = pl.ds(pl.multiple_of(i * 128, 128), 128)
            for j in range(8):
                block = wbuf[which, at, 128 * j : 128 * j + 128]
                target[128 * j : 128 * j + 128, at] = block.T

    d_all().wait_recv()
    low, high = dtgt[0], dtgt[8]
    for s in range(1, 8):
        low, high = low + dtgt[s], high + dtgt[8 + s]
    wanted = jnp.concatenate([low, high], axis=1)
    place = lax.broadcasted_iota(jnp.int32, (TILES, 256), 0) + 1
    onehot[...] = (place == wanted).astype(F32).astype(BF16)

    def aggregate(k):
        nr = ROWS[k]
        got = part(zrecv_a, zrecv_b, k)

        def unpack(s):
            if nr == 16:
                for c in range(CAP):
                    r32[pl.ds(s * 16 + c, 16, stride=256), :] = got[s, c].astype(F32)
            else:
                for c in range(0, CAP, 2):
                    both = got[s, c // 2].astype(F32)
                    r32[pl.ds(s * 16 + c, 8, stride=256), :] = both[:8]
                    r32[pl.ds(s * 16 + c + 1, 8, stride=256), :] = both[8:]

        unpack(n)

        for s, to in zip(senders, receivers):
            z_recv(k, s).wait_recv()
            if k + LOOK < len(ROWS):
                z_send(k + LOOK, to).start()
            unpack(s)

        def rows_of(r):
            return r32[pl.ds(pl.multiple_of(r * 256, 256), 256), :]

        @pl.loop(0, nr // 4)
        def _(quarter):
            for pair in range(2):
                r = quarter * 4 + 2 * pair
                x = jnp.concatenate([rows_of(r), rows_of(r + 1)], axis=1).astype(BF16)
                sums = jnp.dot(onehot[...], x, preferred_element_type=F32)
                g32[pl.ds(r, TILES, stride=nr), :] = sums[:, :128]
                g32[pl.ds(r + 1, TILES, stride=nr), :] = sums[:, 128:]

        def packed(i):
            return g32[pl.ds(pl.multiple_of(i * 8 * nr, 8 * nr), 8 * nr), :].astype(BF16)

        out, mine = part(asend_a, asend_b, k), part(arecv_a, arecv_b, k)
        for to in across:
            out[to] = packed(to)
            g_send(k, to).start()
        mine[f] = packed(f)

    def self_part():
        own_self.wait()
        s_all().wait_recv()

        @pl.loop(0, 4)
        def _(i):
            at = pl.ds(pl.multiple_of(i * 256, 256), 256)
            by8 = [0.0] * B
            for tq in range(2):
                x = srecv[pl.ds(i * 4, 4), :, 512 * tq : 512 * tq + 512].reshape(256, 512)
                moved = lax.dot_general(x, perm[tq], NT, preferred_element_type=F32)
                for k in range(A):
                    selfp_a[k, at, 128 * tq : 128 * tq + 128] = moved[:, 128 * k : 128 * k + 128].astype(BF16)
                for k in range(B):
                    by8[k] = by8[k] + moved[:, 128 * (A + k) : 128 * (A + k) + 128]
            for k in range(B):
                selfp_b[k, at, :] = by8[k].astype(BF16)

        for k in range(A):
            hs_a[k] = jnp.dot(wt1[...], selfp_a[k], preferred_element_type=F32)
        for k in range(B):
            hs_b[k] = jnp.dot(wt1[...], selfp_b[k], preferred_element_type=F32)

    def layer(k):
        nr = ROWS[k]
        wide = 16 * nr
        g_all(k).wait_recv()
        got = part(arecv_a, arecv_b, k)
        lane = lax.broadcasted_iota(jnp.int32, (8 * nr, 128), 1)
        for m in range(8):
            a, b = got[2 * m].astype(F32), got[2 * m + 1].astype(F32)
            first = jnp.where(lane < 64, a, pltpu.roll(b, 64, 1)).astype(BF16)
            second = jnp.where(lane < 64, pltpu.roll(a, 64, 1), b).astype(BF16)
            cols = slice(128 * m, 128 * m + 128)
            for tq in range(2):
                at, of = 8 * nr * tq, slice(4 * nr * tq, 4 * nr * tq + 4 * nr)
                lhs[at : at + 4 * nr, cols] = first[of]
                lhs[at + 4 * nr : at + 8 * nr, cols] = second[of]

        here, away = part(hs_a, hs_b, k), part(bsend_a, bsend_b, k)
        total = jnp.zeros((1, wide), F32)
        for at in range(0, D, D // 2):
            half = slice(at, at + D // 2)
            hidden = here[half] + lax.dot_general(wt0[half], lhs[0:wide], NT, preferred_element_type=F32)
            active = jnp.maximum(hidden, 0.0)
            act[half, 0:wide] = active
            total = total + jnp.sum(active * active, axis=0, keepdims=True)
        scale = lax.rsqrt(total / D + 1e-06)
        for to in across:
            away[rows(to)] = (act[rows(to), 0:wide] * scale).astype(BF16)
            b_send(k, to).start()
        away[rows(f)] = (act[rows(f), 0:wide] * scale).astype(BF16)
        b_own(k).start()

    for step, k in SCHEDULE:
        if step == "sum":
            aggregate(k)
        else:
            if k == 0:
                self_part()
            layer(k)

    for k in range(LAST):
        b_own(k).wait()
        b_all(k).wait_recv()

    def most_copy(i):
        at = pl.ds(pl.multiple_of(i * 4 * SHARE, 4 * SHARE), 4 * SHARE)
        return pltpu.make_async_copy(most.at[:, at], out_most.at[:, at], most_sem.at[i])

    @pl.loop(0, 4)
    def _(i):
        of = pl.ds(pl.multiple_of(i * 256, 256), 256)
        for tq in range(2):
            x = [brecv_a[k, of, 128 * tq : 128 * tq + 128] for k in range(A)] + [brecv_b[k, of, :] for k in range(B - 1)]
            moved = jnp.dot(jnp.concatenate(x, axis=1), perm[tq, 0:MOST], preferred_element_type=F32).astype(BF16)
            for j in range(4):
                at = pl.multiple_of((i * 4 + j) * SHARE + 512 * tq, 512)
                most[:, pl.ds(at, 512)] = moved[C * j : C * j + C]
        most_copy(i).start()

    perm_copy.wait()
    d_all().wait_send()
    s_all().wait_send()
    for k in range(len(ROWS)):
        z_all(k).wait_send()
        g_all(k).wait_send()
        b_all(k).wait_send()
    for i in range(4):
        most_copy(i).wait()
    b_own(LAST).wait()
    b_all(LAST).wait_recv()


def place_kernel(most_ref, last_ref, perm_ref, out_ref, mbuf, lbuf, pbuf, obuf, m_sem, l_sem, p_sem, o_sem):
    def block(i):
        return pl.ds(4 * SHARE * i, 4 * SHARE)

    def fetch(i):
        return pltpu.make_async_copy(most_ref.at[:, block(i)], mbuf.at[i], m_sem.at[i])

    def store(i):
        return pltpu.make_async_copy(obuf.at[i], out_ref.at[:, block(i)], o_sem.at[i])

    fetch_perm = pltpu.make_async_copy(perm_ref, pbuf, p_sem)
    fetch_last = pltpu.make_async_copy(last_ref, lbuf, l_sem)
    fetch_perm.start()
    fetch_last.start()
    for i in range(4):
        fetch(i).start()
    fetch_perm.wait()
    fetch_last.wait()
    for i in range(4):
        fetch(i).wait()
        for tq in range(2):
            moved = jnp.dot(lbuf[256 * i : 256 * i + 256], pbuf[tq], preferred_element_type=F32)
            for j in range(4):
                at = slice(SHARE * j + 512 * tq, SHARE * j + 512 * tq + 512)
                obuf[i, :, at] = (mbuf[i, :, at].astype(F32) + moved[C * j : C * j + C]).astype(BF16)
        store(i).start()
    for i in range(4):
        store(i).wait()


def on_device(features, tile_vals, src_tile, dst_tile, counts, weight):
    hbm = pl.BlockSpec(memory_space=pl.ANY)
    vmem = pl.BlockSpec(memory_space=pltpu.VMEM)
    smem = pl.BlockSpec(memory_space=pltpu.SMEM)
    dma = pltpu.SemaphoreType.DMA
    chunks = len(ROWS)

    def both(rows_a, rows_b, kind=BF16):
        return [pltpu.VMEM((A, *rows_a), kind), pltpu.VMEM((B, *rows_b), kind)]

    most, last, perm = pl.pallas_call(
        kernel,
        out_shape=(
            jax.ShapeDtypeStruct((C, TILES * T), BF16),
            jax.ShapeDtypeStruct((D, 128), BF16),
            jax.ShapeDtypeStruct((2, 128, 512), BF16),
        ),
        in_specs=[smem, vmem, vmem, hbm, hbm, hbm],
        out_specs=(hbm, hbm, hbm),
        scratch_shapes=[
            pltpu.VMEM((C, TILES * T), BF16),
            pltpu.VMEM((TILES, C, T), BF16),
            pltpu.VMEM((N, CAP, T, T), BF16),
            pltpu.VMEM((2, D, D), BF16),
            pltpu.VMEM((D, D), BF16),
            pltpu.VMEM((D, D), BF16),
            *both((N, CAP, 16, 128), (N, CAP // 2, 16, 128)),
            *both((N, CAP, 16, 128), (N, CAP // 2, 16, 128)),
            pltpu.VMEM((128, 128), F32),
            pltpu.VMEM((N, 1, 128), jnp.int32),
            pltpu.VMEM((N, 1, 128), jnp.int32),
            pltpu.VMEM((16 * 256, 128), F32),
            pltpu.VMEM((TILES * 16, 128), F32),
            *both((F, 128, 128), (F, 64, 128)),
            *both((F, 128, 128), (F, 64, 128)),
            pltpu.VMEM((F, C, SHARE), BF16),
            *both((D, 256), (D, 128)),
            *both((D, 256), (D, 128), F32),
            pltpu.VMEM((256, D), BF16),
            pltpu.VMEM((D, 256), F32),
            *both((D, 256), (D, 128)),
            pltpu.VMEM((A, D, 256), BF16),
            pltpu.VMEM((B - 1, D, 128), BF16),
            pltpu.VMEM((C, TILES * T), BF16),
            pltpu.VMEM((2, LANES, 512), BF16),
            pltpu.VMEM((TILES, 256), BF16),
            dma,
            dma((N,)),
            dma,
            dma,
            dma,
            dma((4,)),
            dma((chunks,)),
            dma,
            dma,
            dma,
            dma,
            dma((chunks,)),
            dma((chunks, N)),
            dma((chunks,)),
            dma((chunks,)),
            dma((chunks,)),
            dma((chunks,)),
        ],
        compiler_params=pltpu.CompilerParams(collective_id=1, has_side_effects=True, vmem_limit_bytes=60 * 2**20),
    )(src_tile.transpose(2, 0, 1), dst_tile.transpose(2, 0, 1), counts, features.T, tile_vals[0], weight)
    out = pl.pallas_call(
        place_kernel,
        out_shape=jax.ShapeDtypeStruct((C, TILES * T), BF16),
        in_specs=[hbm, hbm, hbm],
        out_specs=hbm,
        scratch_shapes=[
            pltpu.VMEM((4, C, 4 * SHARE), BF16),
            pltpu.VMEM((D, 128), BF16),
            pltpu.VMEM((2, 128, 512), BF16),
            pltpu.VMEM((4, C, 4 * SHARE), BF16),
            dma((4,)),
            dma,
            dma,
            dma((4,)),
        ],
        compiler_params=pltpu.CompilerParams(vmem_limit_bytes=60 * 2**20),
    )(most, last, perm)
    return out.T


def solution(mesh):
    return jax.shard_map(
        on_device,
        mesh=mesh,
        in_specs=(
            P("nodes", "feat"),
            P("nodes", None, None, None, None),
            P("nodes", None, None),
            P("nodes", None, None),
            P("nodes", None),
            P(),
        ),
        out_specs=P("nodes", "feat"),
        check_vma=False,
    )
```

```python
import jax
import jax.numpy as jnp
from jax import lax
from jax.experimental import pallas as pl
from jax.experimental.pallas import tpu as pltpu
from jax.sharding import PartitionSpec as P

MESH = pl.DeviceIdType.MESH
BF16, F32 = jnp.bfloat16, jnp.float32
N = 16
F = 16
CAP = 12
T = 128
TILES = 128
C = 64
D = 1024
SHARE = 1024
ROWS = (16, 16, 8, 8, 8, 8)
A, B = 2, 4
LOOK = 2
LAST = len(ROWS) - 1
LANES = 128 * (A + B)
MOST = 128 * LAST
SCHEDULE = (
    ("sum", 0), ("layer", 0), ("sum", 1), ("sum", 2), ("layer", 1), ("sum", 3), ("layer", 2),
    ("sum", 4), ("layer", 3), ("layer", 4), ("sum", 5), ("layer", 5),
)

NT = (((1,), (1,)), ((), ()))

FAR = sorted(
    [(dy, dx) for dy in range(4) for dx in range(4) if (dy, dx) != (0, 0)],
    key=lambda o: -(min(o[0], 4 - o[0]) + min(o[1], 4 - o[1])),
)


def node_partner(n, step, sign):
    j = lax.div(step, 2)
    dz = 4 + (2 * lax.rem(j, 2) - 1) * lax.div(j + 1, 2)
    return lax.rem(lax.div(n, 2) + 8 + sign * dz, 8) * 2 + lax.rem(n + step + 1, 2)


def feat_partner(f, offset):
    dy, dx = offset
    return lax.rem(lax.div(f, 4) + dy, 4) * 4 + lax.rem(lax.rem(f, 4) + dx, 4)


def placing(tq):
    lane = lax.broadcasted_iota(jnp.int32, (LANES, 512), 0)
    row = lax.broadcasted_iota(jnp.int32, (LANES, 512), 1)
    tl, h, i = row // 128, (row // 64) % 2, row % 64
    by16 = (i // 16) * 128 + h * 64 + tl * 16 + i % 16
    by8 = A * 128 + ((i - 16 * A) // 8) * 128 + tq * 64 + h * 32 + tl * 8 + i % 8
    return (lane == jnp.where(i < 16 * A, by16, by8)).astype(F32).astype(BF16)


def kernel(
    src_ref,
    dst_ref,
    counts_ref,
    xt_ref,
    a_ref,
    w_ref,
    out_most,
    out_last,
    out_perm,
    xbuf,
    xtile,
    abuf,
    wbuf,
    wt0,
    wt1,
    zsend_a,
    zsend_b,
    zrecv_a,
    zrecv_b,
    turn,
    dmsg,
    dtgt,
    r32,
    g32,
    asend_a,
    asend_b,
    arecv_a,
    arecv_b,
    srecv,
    selfp_a,
    selfp_b,
    hs_a,
    hs_b,
    lhs,
    act,
    bsend_a,
    bsend_b,
    brecv_a,
    brecv_b,
    most,
    perm,
    onehot,
    xsem,
    asem,
    wsem,
    own_sem,
    perm_sem,
    most_sem,
    back_sem,
    d_ss,
    d_rs,
    s_ss,
    s_rs,
    z_ss,
    z_rs,
    g_ss,
    g_rs,
    b_ss,
    b_rs,
):
    n, f = lax.axis_index("nodes"), lax.axis_index("feat")
    across = [feat_partner(f, o) for o in FAR]

    def node(i):
        return (i, f)

    def col(i):
        return (n, i)

    def to_node(step):
        return node_partner(n, step, 1)

    def from_node(step):
        return node_partner(n, step, -1)

    def part(a, b, k):
        return a.at[k] if k < A else b.at[k - A]

    def back(k):
        return out_last if k == LAST else part(brecv_a, brecv_b, k)

    x_copy = pltpu.make_async_copy(xt_ref, xbuf, xsem)
    x_copy.start()

    def a_copy(d):
        return pltpu.make_async_copy(a_ref.at[d], abuf.at[d], asem.at[d])

    @pl.loop(0, 16)
    def _(step):
        a_copy(to_node(step)).start()

    w_copy = pltpu.make_async_copy(w_ref, wbuf, wsem)
    w_copy.start()

    barrier = pltpu.get_barrier_semaphore()

    @pl.loop(0, 15)
    def _(step):
        pl.semaphore_signal(barrier, inc=1, device_id=node(to_node(step)), device_id_type=MESH)

    for to in across:
        pl.semaphore_signal(barrier, inc=1, device_id=col(to), device_id_type=MESH)

    x_copy.wait()

    @pl.loop(0, TILES, unroll=8)
    def _(t):
        xtile[t] = xbuf[:, pl.ds(pl.multiple_of(t * T, T), T)]

    def remote(src, dst, ss, rs, device):
        return pltpu.make_async_remote_copy(src, dst, ss, rs, device_id=device, device_id_type=MESH)

    def all_of(ref, size=1):
        return ref.at[pl.ds(0, 15 * size)]

    def d_send(to):
        return remote(dmsg.at[to], dtgt.at[n], d_ss, d_rs, node(to))

    def d_all():
        return remote(all_of(dmsg), all_of(dtgt), d_ss, d_rs, node(n))

    def share(i):
        return pl.ds(pl.multiple_of(i * SHARE, SHARE), SHARE)

    def s_send(to):
        return remote(xt_ref.at[:, share(to)], srecv.at[f], s_ss, s_rs, col(to))

    def s_all():
        return remote(all_of(srecv), all_of(srecv), s_ss, s_rs, col(f))

    def z_send(k, to):
        src, dst = part(zsend_a, zsend_b, k), part(zrecv_a, zrecv_b, k)
        return remote(src.at[to], dst.at[n], z_ss.at[k], z_rs.at[k, n], node(to))

    def z_recv(k, frm):
        src, dst = part(zsend_a, zsend_b, k), part(zrecv_a, zrecv_b, k)
        return remote(src.at[frm], dst.at[frm], z_ss.at[k], z_rs.at[k, frm], node(frm))

    def z_all(k):
        src, dst = part(zsend_a, zsend_b, k), part(zrecv_a, zrecv_b, k)
        return remote(all_of(src), all_of(dst), z_ss.at[k], z_rs.at[k, n], node(n))

    def g_send(k, to):
        src, dst = part(asend_a, asend_b, k), part(arecv_a, arecv_b, k)
        return remote(src.at[to], dst.at[f], g_ss.at[k], g_rs.at[k], col(to))

    def g_all(k):
        src, dst = part(asend_a, asend_b, k), part(arecv_a, arecv_b, k)
        return remote(all_of(src), all_of(dst), g_ss.at[k], g_rs.at[k], col(f))

    def rows(i):
        return pl.ds(pl.multiple_of(i * C, C), C)

    def b_send(k, to):
        src, dst = part(bsend_a, bsend_b, k), back(k)
        return remote(src.at[rows(to)], dst.at[rows(f)], b_ss.at[k], b_rs.at[k], col(to))

    def b_all(k):
        src, dst = part(bsend_a, bsend_b, k), back(k)
        return remote(all_of(src, C), all_of(dst, C), b_ss.at[k], b_rs.at[k], col(f))

    def b_own(k):
        src, dst = part(bsend_a, bsend_b, k), back(k)
        return pltpu.make_async_copy(src.at[rows(f)], dst.at[rows(f)], back_sem.at[k])

    none = jnp.zeros((C, T), BF16)

    def products(d, to_a, to_b, at):
        kept = None
        for c in range(CAP):
            a = abuf[d, c]
            left = jnp.concatenate([a[: T // 2], a[T // 2 :]], axis=1)
            x = xtile[src_ref[c, 0, d]]
            right = jnp.concatenate(
                [jnp.concatenate([x, none], axis=1), jnp.concatenate([none, x], axis=1)], axis=0
            )
            value = lax.dot_general(left, right, NT, preferred_element_type=F32)
            for k in range(A):
                to_a[k, at, c] = value[16 * k : 16 * k + 16].astype(BF16)
            if c % 2 == 0:
                kept = value
                continue
            for k in range(B):
                rows8 = slice(16 * A + 8 * k, 16 * A + 8 * k + 8)
                to_b[k, at, c // 2] = jnp.concatenate([kept[rows8], value[rows8]], axis=0).astype(BF16)

    def stage_one(step):
        d = to_node(step)
        a_copy(d).wait()
        products(d, zsend_a, zsend_b, d)

    stage_one(0)
    pl.semaphore_wait(barrier, 30)
    z_send(0, to_node(0)).start()

    for to in across:
        s_send(to).start()

    own_self = pltpu.make_async_copy(xt_ref.at[:, share(f)], srecv.at[f], own_sem)
    own_self.start()

    @pl.loop(1, 15)
    def _(step):
        stage_one(step)
        z_send(0, to_node(step)).start()

    turn[...] = jnp.zeros_like(turn)
    for c in range(CAP):
        used = jnp.where(counts_ref[...] > c, dst_ref[c] + 1, 0)
        turn[pl.ds(16 * (n % 8) + c, 1), 0:N] = used.astype(F32)
    turned = turn[...].T
    for d in range(N):
        dmsg[d] = turned[d : d + 1].astype(jnp.int32)

    @pl.loop(0, 15)
    def _(step):
        d_send(to_node(step)).start()

    for k in range(1, LOOK):

        @pl.loop(0, 15)
        def _(step):
            z_send(k, to_node(step)).start()

    a_copy(n).wait()
    products(n, zrecv_a, zrecv_b, n)

    dtgt[n] = dmsg[n]
    r32[...] = jnp.zeros_like(r32)
    perm[0] = placing(0)
    perm[1] = placing(1)
    perm_copy = pltpu.make_async_copy(perm.at[:, pl.ds(MOST, 128)], out_perm, perm_sem)
    perm_copy.start()
    w_copy.wait()

    for which, target in ((0, wt0), (1, wt1)):

        @pl.loop(0, 8)
        def _(i):
            at = pl.ds(pl.multiple_of(i * 128, 128), 128)
            for j in range(8):
                block = wbuf[which, at, 128 * j : 128 * j + 128]
                target[128 * j : 128 * j + 128, at] = block.T

    d_all().wait_recv()
    low, high = dtgt[0], dtgt[8]
    for s in range(1, 8):
        low, high = low + dtgt[s], high + dtgt[8 + s]
    wanted = jnp.concatenate([low, high], axis=1)
    place = lax.broadcasted_iota(jnp.int32, (TILES, 256), 0) + 1
    onehot[...] = (place == wanted).astype(F32).astype(BF16)

    def aggregate(k):
        nr = ROWS[k]
        got = part(zrecv_a, zrecv_b, k)

        def unpack(s):
            if nr == 16:
                for c in range(CAP):
                    r32[pl.ds(s * 16 + c, 16, stride=256), :] = got[s, c].astype(F32)
            else:
                for c in range(0, CAP, 2):
                    both = got[s, c // 2].astype(F32)
                    r32[pl.ds(s * 16 + c, 8, stride=256), :] = both[:8]
                    r32[pl.ds(s * 16 + c + 1, 8, stride=256), :] = both[8:]

        unpack(n)

        @pl.loop(0, 15)
        def _(step):
            s = from_node(step)
            z_recv(k, s).wait_recv()
            if k + LOOK < len(ROWS):
                z_send(k + LOOK, to_node(step)).start()
            unpack(s)

        def rows_of(r):
            return r32[pl.ds(pl.multiple_of(r * 256, 256), 256), :]

        @pl.loop(0, nr // 4)
        def _(quarter):
            for pair in range(2):
                r = quarter * 4 + 2 * pair
                x = jnp.concatenate([rows_of(r), rows_of(r + 1)], axis=1).astype(BF16)
                sums = jnp.dot(onehot[...], x, preferred_element_type=F32)
                g32[pl.ds(r, TILES, stride=nr), :] = sums[:, :128]
                g32[pl.ds(r + 1, TILES, stride=nr), :] = sums[:, 128:]

        def packed(i):
            return g32[pl.ds(pl.multiple_of(i * 8 * nr, 8 * nr), 8 * nr), :].astype(BF16)

        out, mine = part(asend_a, asend_b, k), part(arecv_a, arecv_b, k)
        for to in across:
            out[to] = packed(to)
            g_send(k, to).start()
        mine[f] = packed(f)

    def self_part():
        own_self.wait()
        s_all().wait_recv()

        @pl.loop(0, 4)
        def _(i):
            at = pl.ds(pl.multiple_of(i * 256, 256), 256)
            by8 = [0.0] * B
            for tq in range(2):
                x = srecv[pl.ds(i * 4, 4), :, 512 * tq : 512 * tq + 512].reshape(256, 512)
                moved = lax.dot_general(x, perm[tq], NT, preferred_element_type=F32)
                for k in range(A):
                    selfp_a[k, at, 128 * tq : 128 * tq + 128] = moved[:, 128 * k : 128 * k + 128].astype(BF16)
                for k in range(B):
                    by8[k] = by8[k] + moved[:, 128 * (A + k) : 128 * (A + k) + 128]
            for k in range(B):
                selfp_b[k, at, :] = by8[k].astype(BF16)

        for k in range(A):
            hs_a[k] = jnp.dot(wt1[...], selfp_a[k], preferred_element_type=F32)
        for k in range(B):
            hs_b[k] = jnp.dot(wt1[...], selfp_b[k], preferred_element_type=F32)

    def layer(k):
        nr = ROWS[k]
        wide = 16 * nr
        g_all(k).wait_recv()
        got = part(arecv_a, arecv_b, k)
        lane = lax.broadcasted_iota(jnp.int32, (8 * nr, 128), 1)
        for m in range(8):
            a, b = got[2 * m].astype(F32), got[2 * m + 1].astype(F32)
            first = jnp.where(lane < 64, a, pltpu.roll(b, 64, 1)).astype(BF16)
            second = jnp.where(lane < 64, pltpu.roll(a, 64, 1), b).astype(BF16)
            cols = slice(128 * m, 128 * m + 128)
            for tq in range(2):
                at, of = 8 * nr * tq, slice(4 * nr * tq, 4 * nr * tq + 4 * nr)
                lhs[at : at + 4 * nr, cols] = first[of]
                lhs[at + 4 * nr : at + 8 * nr, cols] = second[of]

        here, away = part(hs_a, hs_b, k), part(bsend_a, bsend_b, k)
        total = jnp.zeros((1, wide), F32)
        for at in range(0, D, D // 2):
            half = slice(at, at + D // 2)
            hidden = here[half] + lax.dot_general(wt0[half], lhs[0:wide], NT, preferred_element_type=F32)
            active = jnp.maximum(hidden, 0.0)
            act[half, 0:wide] = active
            total = total + jnp.sum(active * active, axis=0, keepdims=True)
        scale = lax.rsqrt(total / D + 1e-06)
        for to in across:
            away[rows(to)] = (act[rows(to), 0:wide] * scale).astype(BF16)
            b_send(k, to).start()
        away[rows(f)] = (act[rows(f), 0:wide] * scale).astype(BF16)
        b_own(k).start()

    for step, k in SCHEDULE:
        if step == "sum":
            aggregate(k)
        else:
            if k == 0:
                self_part()
            layer(k)

    for k in range(LAST):
        b_own(k).wait()
        b_all(k).wait_recv()

    def most_copy(i):
        at = pl.ds(pl.multiple_of(i * 4 * SHARE, 4 * SHARE), 4 * SHARE)
        return pltpu.make_async_copy(most.at[:, at], out_most.at[:, at], most_sem.at[i])

    @pl.loop(0, 4)
    def _(i):
        of = pl.ds(pl.multiple_of(i * 256, 256), 256)
        for tq in range(2):
            x = [brecv_a[k, of, 128 * tq : 128 * tq + 128] for k in range(A)] + [brecv_b[k, of, :] for k in range(B - 1)]
            moved = jnp.dot(jnp.concatenate(x, axis=1), perm[tq, 0:MOST], preferred_element_type=F32).astype(BF16)
            for j in range(4):
                at = pl.multiple_of((i * 4 + j) * SHARE + 512 * tq, 512)
                most[:, pl.ds(at, 512)] = moved[C * j : C * j + C]
        most_copy(i).start()

    perm_copy.wait()
    d_all().wait_send()
    s_all().wait_send()
    for k in range(len(ROWS)):
        z_all(k).wait_send()
        g_all(k).wait_send()
        b_all(k).wait_send()
    for i in range(4):
        most_copy(i).wait()
    b_own(LAST).wait()
    b_all(LAST).wait_recv()


def place_kernel(most_ref, last_ref, perm_ref, out_ref, mbuf, lbuf, pbuf, obuf, m_sem, l_sem, p_sem, o_sem):
    def block(i):
        return pl.ds(4 * SHARE * i, 4 * SHARE)

    def fetch(i):
        return pltpu.make_async_copy(most_ref.at[:, block(i)], mbuf.at[i], m_sem.at[i])

    def store(i):
        return pltpu.make_async_copy(obuf.at[i], out_ref.at[:, block(i)], o_sem.at[i])

    fetch_perm = pltpu.make_async_copy(perm_ref, pbuf, p_sem)
    fetch_last = pltpu.make_async_copy(last_ref, lbuf, l_sem)
    fetch_perm.start()
    fetch_last.start()
    for i in range(4):
        fetch(i).start()
    fetch_perm.wait()
    fetch_last.wait()
    for i in range(4):
        fetch(i).wait()
        for tq in range(2):
            moved = jnp.dot(lbuf[256 * i : 256 * i + 256], pbuf[tq], preferred_element_type=F32)
            for j in range(4):
                at = slice(SHARE * j + 512 * tq, SHARE * j + 512 * tq + 512)
                obuf[i, :, at] = (mbuf[i, :, at].astype(F32) + moved[C * j : C * j + C]).astype(BF16)
        store(i).start()
    for i in range(4):
        store(i).wait()


def on_device(features, tile_vals, src_tile, dst_tile, counts, weight):
    hbm = pl.BlockSpec(memory_space=pl.ANY)
    vmem = pl.BlockSpec(memory_space=pltpu.VMEM)
    smem = pl.BlockSpec(memory_space=pltpu.SMEM)
    dma = pltpu.SemaphoreType.DMA
    chunks = len(ROWS)

    def both(rows_a, rows_b, kind=BF16):
        return [pltpu.VMEM((A, *rows_a), kind), pltpu.VMEM((B, *rows_b), kind)]

    most, last, perm = pl.pallas_call(
        kernel,
        out_shape=(
            jax.ShapeDtypeStruct((C, TILES * T), BF16),
            jax.ShapeDtypeStruct((D, 128), BF16),
            jax.ShapeDtypeStruct((2, 128, 512), BF16),
        ),
        in_specs=[smem, vmem, vmem, hbm, hbm, hbm],
        out_specs=(hbm, hbm, hbm),
        scratch_shapes=[
            pltpu.VMEM((C, TILES * T), BF16),
            pltpu.VMEM((TILES, C, T), BF16),
            pltpu.VMEM((N, CAP, T, T), BF16),
            pltpu.VMEM((2, D, D), BF16),
            pltpu.VMEM((D, D), BF16),
            pltpu.VMEM((D, D), BF16),
            *both((N, CAP, 16, 128), (N, CAP // 2, 16, 128)),
            *both((N, CAP, 16, 128), (N, CAP // 2, 16, 128)),
            pltpu.VMEM((128, 128), F32),
            pltpu.VMEM((N, 1, 128), jnp.int32),
            pltpu.VMEM((N, 1, 128), jnp.int32),
            pltpu.VMEM((16 * 256, 128), F32),
            pltpu.VMEM((TILES * 16, 128), F32),
            *both((F, 128, 128), (F, 64, 128)),
            *both((F, 128, 128), (F, 64, 128)),
            pltpu.VMEM((F, C, SHARE), BF16),
            *both((D, 256), (D, 128)),
            *both((D, 256), (D, 128), F32),
            pltpu.VMEM((256, D), BF16),
            pltpu.VMEM((D, 256), F32),
            *both((D, 256), (D, 128)),
            pltpu.VMEM((A, D, 256), BF16),
            pltpu.VMEM((B - 1, D, 128), BF16),
            pltpu.VMEM((C, TILES * T), BF16),
            pltpu.VMEM((2, LANES, 512), BF16),
            pltpu.VMEM((TILES, 256), BF16),
            dma,
            dma((N,)),
            dma,
            dma,
            dma,
            dma((4,)),
            dma((chunks,)),
            dma,
            dma,
            dma,
            dma,
            dma((chunks,)),
            dma((chunks, N)),
            dma((chunks,)),
            dma((chunks,)),
            dma((chunks,)),
            dma((chunks,)),
        ],
        compiler_params=pltpu.CompilerParams(collective_id=1, has_side_effects=True, vmem_limit_bytes=60 * 2**20),
    )(src_tile.transpose(2, 0, 1), dst_tile.transpose(2, 0, 1), counts, features.T, tile_vals[0], weight)
    out = pl.pallas_call(
        place_kernel,
        out_shape=jax.ShapeDtypeStruct((C, TILES * T), BF16),
        in_specs=[hbm, hbm, hbm],
        out_specs=hbm,
        scratch_shapes=[
            pltpu.VMEM((4, C, 4 * SHARE), BF16),
            pltpu.VMEM((D, 128), BF16),
            pltpu.VMEM((2, 128, 512), BF16),
            pltpu.VMEM((4, C, 4 * SHARE), BF16),
            dma((4,)),
            dma,
            dma,
            dma((4,)),
        ],
        compiler_params=pltpu.CompilerParams(vmem_limit_bytes=60 * 2**20),
    )(most, last, perm)
    return out.T


def solution(mesh):
    return jax.shard_map(
        on_device,
        mesh=mesh,
        in_specs=(
            P("nodes", "feat"),
            P("nodes", None, None, None, None),
            P("nodes", None, None),
            P("nodes", None, None),
            P("nodes", None),
            P(),
        ),
        out_specs=P("nodes", "feat"),
        check_vma=False,
    )
```

```python
import jax
import jax.numpy as jnp
from jax import lax
from jax.experimental import pallas as pl
from jax.experimental.pallas import tpu as pltpu
from jax.sharding import PartitionSpec as P

MESH = pl.DeviceIdType.MESH
BF16, F32 = jnp.bfloat16, jnp.float32
N = 16
F = 16
CAP = 12
T = 128
TILES = 128
C = 64
D = 1024
SHARE = 1024
ROWS = (16, 16, 8, 8, 8, 8)
A, B = 2, 4
LOOK = 2
LAST = len(ROWS) - 1
LANES = 128 * (A + B)
MOST = 128 * LAST
SCHEDULE = (
    ("sum", 0), ("layer", 0), ("sum", 1), ("sum", 2), ("layer", 1), ("sum", 3), ("layer", 2),
    ("sum", 4), ("layer", 3), ("sum", 5), ("layer", 4), ("layer", 5),
)

NT = (((1,), (1,)), ((), ()))

FAR = sorted(
    [(dy, dx) for dy in range(4) for dx in range(4) if (dy, dx) != (0, 0)],
    key=lambda o: -(min(o[0], 4 - o[0]) + min(o[1], 4 - o[1])),
)


def node_partner(n, step, sign):
    j = lax.div(step, 2)
    dz = 4 + (2 * lax.rem(j, 2) - 1) * lax.div(j + 1, 2)
    return lax.rem(lax.div(n, 2) + 8 + sign * dz, 8) * 2 + lax.rem(n + step + 1, 2)


def feat_partner(f, offset):
    dy, dx = offset
    return lax.rem(lax.div(f, 4) + dy, 4) * 4 + lax.rem(lax.rem(f, 4) + dx, 4)


def placing(tq):
    lane = lax.broadcasted_iota(jnp.int32, (LANES, 512), 0)
    row = lax.broadcasted_iota(jnp.int32, (LANES, 512), 1)
    tl, h, i = row // 128, (row // 64) % 2, row % 64
    by16 = (i // 16) * 128 + h * 64 + tl * 16 + i % 16
    by8 = A * 128 + ((i - 16 * A) // 8) * 128 + tq * 64 + h * 32 + tl * 8 + i % 8
    return (lane == jnp.where(i < 16 * A, by16, by8)).astype(F32).astype(BF16)


def kernel(
    src_ref,
    dst_ref,
    counts_ref,
    xt_ref,
    a_ref,
    w_ref,
    out_most,
    out_last,
    out_perm,
    xbuf,
    xtile,
    abuf,
    wbuf,
    wt0,
    wt1,
    zsend_a,
    zsend_b,
    zrecv_a,
    zrecv_b,
    turn,
    dmsg,
    dtgt,
    r32,
    g32,
    asend_a,
    asend_b,
    arecv_a,
    arecv_b,
    srecv,
    selfp_a,
    selfp_b,
    hs_a,
    hs_b,
    lhs,
    act,
    bsend_a,
    bsend_b,
    brecv_a,
    brecv_b,
    most,
    perm,
    onehot,
    xsem,
    asem,
    wsem,
    own_sem,
    perm_sem,
    most_sem,
    back_sem,
    d_ss,
    d_rs,
    s_ss,
    s_rs,
    z_ss,
    z_rs,
    g_ss,
    g_rs,
    b_ss,
    b_rs,
):
    n, f = lax.axis_index("nodes"), lax.axis_index("feat")
    across = [feat_partner(f, o) for o in FAR]

    def node(i):
        return (i, f)

    def col(i):
        return (n, i)

    def to_node(step):
        return node_partner(n, step, 1)

    def from_node(step):
        return node_partner(n, step, -1)

    def part(a, b, k):
        return a.at[k] if k < A else b.at[k - A]

    def back(k):
        return out_last if k == LAST else part(brecv_a, brecv_b, k)

    x_copy = pltpu.make_async_copy(xt_ref, xbuf, xsem)
    x_copy.start()

    def a_copy(d):
        return pltpu.make_async_copy(a_ref.at[d], abuf.at[d], asem.at[d])

    @pl.loop(0, 16)
    def _(step):
        a_copy(to_node(step)).start()

    w_copy = pltpu.make_async_copy(w_ref, wbuf, wsem)
    w_copy.start()

    barrier = pltpu.get_barrier_semaphore()

    @pl.loop(0, 15)
    def _(step):
        pl.semaphore_signal(barrier, inc=1, device_id=node(to_node(step)), device_id_type=MESH)

    for to in across:
        pl.semaphore_signal(barrier, inc=1, device_id=col(to), device_id_type=MESH)

    x_copy.wait()

    @pl.loop(0, TILES, unroll=8)
    def _(t):
        xtile[t] = xbuf[:, pl.ds(pl.multiple_of(t * T, T), T)]

    def remote(src, dst, ss, rs, device):
        return pltpu.make_async_remote_copy(src, dst, ss, rs, device_id=device, device_id_type=MESH)

    def all_of(ref, size=1):
        return ref.at[pl.ds(0, 15 * size)]

    def d_send(to):
        return remote(dmsg.at[to], dtgt.at[n], d_ss, d_rs, node(to))

    def d_all():
        return remote(all_of(dmsg), all_of(dtgt), d_ss, d_rs, node(n))

    def share(i):
        return pl.ds(pl.multiple_of(i * SHARE, SHARE), SHARE)

    def s_send(to):
        return remote(xt_ref.at[:, share(to)], srecv.at[f], s_ss, s_rs, col(to))

    def s_all():
        return remote(all_of(srecv), all_of(srecv), s_ss, s_rs, col(f))

    def z_send(k, to):
        src, dst = part(zsend_a, zsend_b, k), part(zrecv_a, zrecv_b, k)
        return remote(src.at[to], dst.at[n], z_ss.at[k], z_rs.at[k, n], node(to))

    def z_recv(k, frm):
        src, dst = part(zsend_a, zsend_b, k), part(zrecv_a, zrecv_b, k)
        return remote(src.at[frm], dst.at[frm], z_ss.at[k], z_rs.at[k, frm], node(frm))

    def z_all(k):
        src, dst = part(zsend_a, zsend_b, k), part(zrecv_a, zrecv_b, k)
        return remote(all_of(src), all_of(dst), z_ss.at[k], z_rs.at[k, n], node(n))

    def g_send(k, to):
        src, dst = part(asend_a, asend_b, k), part(arecv_a, arecv_b, k)
        return remote(src.at[to], dst.at[f], g_ss.at[k], g_rs.at[k], col(to))

    def g_all(k):
        src, dst = part(asend_a, asend_b, k), part(arecv_a, arecv_b, k)
        return remote(all_of(src), all_of(dst), g_ss.at[k], g_rs.at[k], col(f))

    def rows(i):
        return pl.ds(pl.multiple_of(i * C, C), C)

    def b_send(k, to):
        src, dst = part(bsend_a, bsend_b, k), back(k)
        return remote(src.at[rows(to)], dst.at[rows(f)], b_ss.at[k], b_rs.at[k], col(to))

    def b_all(k):
        src, dst = part(bsend_a, bsend_b, k), back(k)
        return remote(all_of(src, C), all_of(dst, C), b_ss.at[k], b_rs.at[k], col(f))

    def b_own(k):
        src, dst = part(bsend_a, bsend_b, k), back(k)
        return pltpu.make_async_copy(src.at[rows(f)], dst.at[rows(f)], back_sem.at[k])

    none = jnp.zeros((C, T), BF16)

    def products(d, to_a, to_b, at):
        kept = None
        for c in range(CAP):
            a = abuf[d, c]
            left = jnp.concatenate([a[: T // 2], a[T // 2 :]], axis=1)
            x = xtile[src_ref[c, 0, d]]
            right = jnp.concatenate(
                [jnp.concatenate([x, none], axis=1), jnp.concatenate([none, x], axis=1)], axis=0
            )
            value = lax.dot_general(left, right, NT, preferred_element_type=F32)
            for k in range(A):
                to_a[k, at, c] = value[16 * k : 16 * k + 16].astype(BF16)
            if c % 2 == 0:
                kept = value
                continue
            for k in range(B):
                rows8 = slice(16 * A + 8 * k, 16 * A + 8 * k + 8)
                to_b[k, at, c // 2] = jnp.concatenate([kept[rows8], value[rows8]], axis=0).astype(BF16)

    def stage_one(step):
        d = to_node(step)
        a_copy(d).wait()
        products(d, zsend_a, zsend_b, d)

    stage_one(0)
    pl.semaphore_wait(barrier, 30)
    z_send(0, to_node(0)).start()

    for to in across:
        s_send(to).start()

    own_self = pltpu.make_async_copy(xt_ref.at[:, share(f)], srecv.at[f], own_sem)
    own_self.start()

    @pl.loop(1, 15)
    def _(step):
        stage_one(step)
        z_send(0, to_node(step)).start()

    turn[...] = jnp.zeros_like(turn)
    for c in range(CAP):
        used = jnp.where(counts_ref[...] > c, dst_ref[c] + 1, 0)
        turn[pl.ds(16 * (n % 8) + c, 1), 0:N] = used.astype(F32)
    turned = turn[...].T
    for d in range(N):
        dmsg[d] = turned[d : d + 1].astype(jnp.int32)

    @pl.loop(0, 15)
    def _(step):
        d_send(to_node(step)).start()

    for k in range(1, LOOK):

        @pl.loop(0, 15)
        def _(step):
            z_send(k, to_node(step)).start()

    a_copy(n).wait()
    products(n, zrecv_a, zrecv_b, n)

    dtgt[n] = dmsg[n]
    r32[...] = jnp.zeros_like(r32)
    perm[0] = placing(0)
    perm[1] = placing(1)
    perm_copy = pltpu.make_async_copy(perm.at[:, pl.ds(MOST, 128)], out_perm, perm_sem)
    perm_copy.start()
    w_copy.wait()

    for which, target in ((0, wt0), (1, wt1)):

        @pl.loop(0, 8)
        def _(i):
            at = pl.ds(pl.multiple_of(i * 128, 128), 128)
            for j in range(8):
                block = wbuf[which, at, 128 * j : 128 * j + 128]
                target[128 * j : 128 * j + 128, at] = block.T

    d_all().wait_recv()
    low, high = dtgt[0], dtgt[8]
    for s in range(1, 8):
        low, high = low + dtgt[s], high + dtgt[8 + s]
    wanted = jnp.concatenate([low, high], axis=1)
    place = lax.broadcasted_iota(jnp.int32, (TILES, 256), 0) + 1
    onehot[...] = (place == wanted).astype(F32).astype(BF16)

    def aggregate(k):
        nr = ROWS[k]
        got = part(zrecv_a, zrecv_b, k)

        def unpack(s):
            if nr == 16:
                for c in range(CAP):
                    r32[pl.ds(s * 16 + c, 16, stride=256), :] = got[s, c].astype(F32)
            else:
                for c in range(0, CAP, 2):
                    both = got[s, c // 2].astype(F32)
                    r32[pl.ds(s * 16 + c, 8, stride=256), :] = both[:8]
                    r32[pl.ds(s * 16 + c + 1, 8, stride=256), :] = both[8:]

        unpack(n)

        @pl.loop(0, 15)
        def _(step):
            s = from_node(step)
            z_recv(k, s).wait_recv()
            if k + LOOK < len(ROWS):
                z_send(k + LOOK, to_node(step)).start()
            unpack(s)

        def rows_of(r):
            return r32[pl.ds(pl.multiple_of(r * 256, 256), 256), :]

        @pl.loop(0, nr // 4)
        def _(quarter):
            for pair in range(2):
                r = quarter * 4 + 2 * pair
                x = jnp.concatenate([rows_of(r), rows_of(r + 1)], axis=1).astype(BF16)
                sums = jnp.dot(onehot[...], x, preferred_element_type=F32)
                g32[pl.ds(r, TILES, stride=nr), :] = sums[:, :128]
                g32[pl.ds(r + 1, TILES, stride=nr), :] = sums[:, 128:]

        def packed(i):
            return g32[pl.ds(pl.multiple_of(i * 8 * nr, 8 * nr), 8 * nr), :].astype(BF16)

        out, mine = part(asend_a, asend_b, k), part(arecv_a, arecv_b, k)
        for to in across:
            out[to] = packed(to)
            g_send(k, to).start()
        mine[f] = packed(f)

    def self_part():
        own_self.wait()
        s_all().wait_recv()

        @pl.loop(0, 4)
        def _(i):
            at = pl.ds(pl.multiple_of(i * 256, 256), 256)
            by8 = [0.0] * B
            for tq in range(2):
                x = srecv[pl.ds(i * 4, 4), :, 512 * tq : 512 * tq + 512].reshape(256, 512)
                moved = lax.dot_general(x, perm[tq], NT, preferred_element_type=F32)
                for k in range(A):
                    selfp_a[k, at, 128 * tq : 128 * tq + 128] = moved[:, 128 * k : 128 * k + 128].astype(BF16)
                for k in range(B):
                    by8[k] = by8[k] + moved[:, 128 * (A + k) : 128 * (A + k) + 128]
            for k in range(B):
                selfp_b[k, at, :] = by8[k].astype(BF16)

        for k in range(A):
            hs_a[k] = jnp.dot(wt1[...], selfp_a[k], preferred_element_type=F32)
        for k in range(B):
            hs_b[k] = jnp.dot(wt1[...], selfp_b[k], preferred_element_type=F32)

    def layer(k):
        nr = ROWS[k]
        wide = 16 * nr
        g_all(k).wait_recv()
        got = part(arecv_a, arecv_b, k)
        lane = lax.broadcasted_iota(jnp.int32, (8 * nr, 128), 1)
        for m in range(8):
            a, b = got[2 * m].astype(F32), got[2 * m + 1].astype(F32)
            first = jnp.where(lane < 64, a, pltpu.roll(b, 64, 1)).astype(BF16)
            second = jnp.where(lane < 64, pltpu.roll(a, 64, 1), b).astype(BF16)
            cols = slice(128 * m, 128 * m + 128)
            for tq in range(2):
                at, of = 8 * nr * tq, slice(4 * nr * tq, 4 * nr * tq + 4 * nr)
                lhs[at : at + 4 * nr, cols] = first[of]
                lhs[at + 4 * nr : at + 8 * nr, cols] = second[of]

        here, away = part(hs_a, hs_b, k), part(bsend_a, bsend_b, k)
        total = jnp.zeros((1, wide), F32)
        for at in range(0, D, D // 2):
            half = slice(at, at + D // 2)
            hidden = here[half] + lax.dot_general(wt0[half], lhs[0:wide], NT, preferred_element_type=F32)
            active = jnp.maximum(hidden, 0.0)
            act[half, 0:wide] = active
            total = total + jnp.sum(active * active, axis=0, keepdims=True)
        scale = lax.rsqrt(total / D + 1e-06)
        for to in across:
            away[rows(to)] = (act[rows(to), 0:wide] * scale).astype(BF16)
            b_send(k, to).start()
        away[rows(f)] = (act[rows(f), 0:wide] * scale).astype(BF16)
        b_own(k).start()

    for step, k in SCHEDULE:
        if step == "sum":
            aggregate(k)
        else:
            if k == 0:
                self_part()
            layer(k)

    for k in range(LAST):
        b_own(k).wait()
        b_all(k).wait_recv()

    def most_copy(i):
        at = pl.ds(pl.multiple_of(i * 4 * SHARE, 4 * SHARE), 4 * SHARE)
        return pltpu.make_async_copy(most.at[:, at], out_most.at[:, at], most_sem.at[i])

    @pl.loop(0, 4)
    def _(i):
        of = pl.ds(pl.multiple_of(i * 256, 256), 256)
        for tq in range(2):
            x = [brecv_a[k, of, 128 * tq : 128 * tq + 128] for k in range(A)] + [brecv_b[k, of, :] for k in range(B - 1)]
            moved = jnp.dot(jnp.concatenate(x, axis=1), perm[tq, 0:MOST], preferred_element_type=F32).astype(BF16)
            for j in range(4):
                at = pl.multiple_of((i * 4 + j) * SHARE + 512 * tq, 512)
                most[:, pl.ds(at, 512)] = moved[C * j : C * j + C]
        most_copy(i).start()

    perm_copy.wait()
    d_all().wait_send()
    s_all().wait_send()
    for k in range(len(ROWS)):
        z_all(k).wait_send()
        g_all(k).wait_send()
        b_all(k).wait_send()
    for i in range(4):
        most_copy(i).wait()
    b_own(LAST).wait()
    b_all(LAST).wait_recv()


def place_kernel(most_ref, last_ref, perm_ref, out_ref, mbuf, lbuf, pbuf, obuf, m_sem, l_sem, p_sem, o_sem):
    def block(i):
        return pl.ds(4 * SHARE * i, 4 * SHARE)

    def fetch(i):
        return pltpu.make_async_copy(most_ref.at[:, block(i)], mbuf.at[i], m_sem.at[i])

    def store(i):
        return pltpu.make_async_copy(obuf.at[i], out_ref.at[:, block(i)], o_sem.at[i])

    fetch_perm = pltpu.make_async_copy(perm_ref, pbuf, p_sem)
    fetch_last = pltpu.make_async_copy(last_ref, lbuf, l_sem)
    fetch_perm.start()
    fetch_last.start()
    for i in range(4):
        fetch(i).start()
    fetch_perm.wait()
    fetch_last.wait()
    for i in range(4):
        fetch(i).wait()
        for tq in range(2):
            moved = jnp.dot(lbuf[256 * i : 256 * i + 256], pbuf[tq], preferred_element_type=F32)
            for j in range(4):
                at = slice(SHARE * j + 512 * tq, SHARE * j + 512 * tq + 512)
                obuf[i, :, at] = (mbuf[i, :, at].astype(F32) + moved[C * j : C * j + C]).astype(BF16)
        store(i).start()
    for i in range(4):
        store(i).wait()


def on_device(features, tile_vals, src_tile, dst_tile, counts, weight):
    hbm = pl.BlockSpec(memory_space=pl.ANY)
    vmem = pl.BlockSpec(memory_space=pltpu.VMEM)
    smem = pl.BlockSpec(memory_space=pltpu.SMEM)
    dma = pltpu.SemaphoreType.DMA
    chunks = len(ROWS)

    def both(rows_a, rows_b, kind=BF16):
        return [pltpu.VMEM((A, *rows_a), kind), pltpu.VMEM((B, *rows_b), kind)]

    most, last, perm = pl.pallas_call(
        kernel,
        out_shape=(
            jax.ShapeDtypeStruct((C, TILES * T), BF16),
            jax.ShapeDtypeStruct((D, 128), BF16),
            jax.ShapeDtypeStruct((2, 128, 512), BF16),
        ),
        in_specs=[smem, vmem, vmem, hbm, hbm, hbm],
        out_specs=(hbm, hbm, hbm),
        scratch_shapes=[
            pltpu.VMEM((C, TILES * T), BF16),
            pltpu.VMEM((TILES, C, T), BF16),
            pltpu.VMEM((N, CAP, T, T), BF16),
            pltpu.VMEM((2, D, D), BF16),
            pltpu.VMEM((D, D), BF16),
            pltpu.VMEM((D, D), BF16),
            *both((N, CAP, 16, 128), (N, CAP // 2, 16, 128)),
            *both((N, CAP, 16, 128), (N, CAP // 2, 16, 128)),
            pltpu.VMEM((128, 128), F32),
            pltpu.VMEM((N, 1, 128), jnp.int32),
            pltpu.VMEM((N, 1, 128), jnp.int32),
            pltpu.VMEM((16 * 256, 128), F32),
            pltpu.VMEM((TILES * 16, 128), F32),
            *both((F, 128, 128), (F, 64, 128)),
            *both((F, 128, 128), (F, 64, 128)),
            pltpu.VMEM((F, C, SHARE), BF16),
            *both((D, 256), (D, 128)),
            *both((D, 256), (D, 128), F32),
            pltpu.VMEM((256, D), BF16),
            pltpu.VMEM((D, 256), F32),
            *both((D, 256), (D, 128)),
            pltpu.VMEM((A, D, 256), BF16),
            pltpu.VMEM((B - 1, D, 128), BF16),
            pltpu.VMEM((C, TILES * T), BF16),
            pltpu.VMEM((2, LANES, 512), BF16),
            pltpu.VMEM((TILES, 256), BF16),
            dma,
            dma((N,)),
            dma,
            dma,
            dma,
            dma((4,)),
            dma((chunks,)),
            dma,
            dma,
            dma,
            dma,
            dma((chunks,)),
            dma((chunks, N)),
            dma((chunks,)),
            dma((chunks,)),
            dma((chunks,)),
            dma((chunks,)),
        ],
        compiler_params=pltpu.CompilerParams(collective_id=1, has_side_effects=True, vmem_limit_bytes=60 * 2**20),
    )(src_tile.transpose(2, 0, 1), dst_tile.transpose(2, 0, 1), counts, features.T, tile_vals[0], weight)
    out = pl.pallas_call(
        place_kernel,
        out_shape=jax.ShapeDtypeStruct((C, TILES * T), BF16),
        in_specs=[hbm, hbm, hbm],
        out_specs=hbm,
        scratch_shapes=[
            pltpu.VMEM((4, C, 4 * SHARE), BF16),
            pltpu.VMEM((D, 128), BF16),
            pltpu.VMEM((2, 128, 512), BF16),
            pltpu.VMEM((4, C, 4 * SHARE), BF16),
            dma((4,)),
            dma,
            dma,
            dma((4,)),
        ],
        compiler_params=pltpu.CompilerParams(vmem_limit_bytes=60 * 2**20),
    )(most, last, perm)
    return out.T


def solution(mesh):
    return jax.shard_map(
        on_device,
        mesh=mesh,
        in_specs=(
            P("nodes", "feat"),
            P("nodes", None, None, None, None),
            P("nodes", None, None),
            P("nodes", None, None),
            P("nodes", None),
            P(),
        ),
        out_specs=P("nodes", "feat"),
        check_vma=False,
    )
```
